32 devices in a mesh: row: 4 (over y, core), col: 8 (over z, x).
Axes of the slice: x: 2, y: 2, z: 4, core: 2. Of those that a mesh axis runs over, the one named last changes fastest.
Arguments:
- features: bfloat16 [16384, 256], P(('col', 'row')), may hold values from -6 to 6
- weight: bfloat16 [256, 256], replicated, may hold values from -0.375 to 0.375
- tile_coords: int32 [4, 8, 144, 2], P('row', 'col'), may hold values from 0 to 31, as said below
- tile_live: int32 [4, 8], P('row', 'col'), may hold values from 36 to 144, as said below
- tile_edges: int32 [4, 8, 144, 128, 128], P('row', 'col'), may hold values 0 or 1
- row_degree: int32 [16384], P(('row', 'col')), may hold values from 1 to 64
- col_degree: int32 [16384], P(('col', 'row')), may hold values from 1 to 64
- cotangent: bfloat16 [16384, 256], P(('row', 'col')), may hold values from -6 to 6
Outputs:
- aggregated: bfloat16 [16384, 256], P(('row', 'col'))
- grad_features: bfloat16 [16384, 256], P(('col', 'row'))
- grad_weight: float32 [256, 256], replicated
The draws below stay inside these ranges and needn't reach their ends.
Inputs may be any that keep to these rules, and one draw needn't show every extreme that they name: `tile_coords`: entry 0 of a slot is a row tile of the block, 0 to 31, entry 1 a column tile, 0 to 15; slots naming the same position add. `tile_live`: the number of live leading slots of each block's list; some block fills all 144 slots.
All inputs are finite; a program needn't handle non-finite values. No bound on the sum of `tile_edges` on one device may be relied on, other than what follows from the above.
Results may differ from the reference program's by a relative error of at most 0.0055.
Values may be sent and summed in bfloat16 or wider, within the bound.
A program may use at most 128 MiB of HBM per device.

```python
import jax
import jax.numpy as jnp
from jax import lax

F = 256
TILE = 128
COL_TILES = 16
TILES_DEV = 144
NODES = 16384
ROW_TILES = 32
N_ROW = 4
N_COL = 8


def draw_tile_coords(key, part):
    key = jax.random.fold_in(key, 11)
    first_key, second_key = jax.random.split(key)
    row_tiles = jax.random.randint(first_key, (N_ROW, N_COL, TILES_DEV, 1), 0, ROW_TILES)
    col_tiles = jax.random.randint(second_key, (N_ROW, N_COL, TILES_DEV, 1), 0, COL_TILES)
    return jnp.concatenate([row_tiles, col_tiles], axis=3).astype(jnp.int32)


def draw_tile_live(key, part):
    key = jax.random.fold_in(key, 23)
    count_key, full_key, least_key = jax.random.split(key, 3)
    blocks = N_ROW * N_COL
    counts = jax.random.randint(count_key, (blocks,), TILES_DEV // 4, TILES_DEV + 1)
    full_at = jax.random.randint(full_key, (), 0, blocks)
    least_at = (full_at + 1 + jax.random.randint(least_key, (), 0, blocks - 1)) % blocks
    places = jnp.arange(blocks)
    counts = jnp.where(places == full_at, TILES_DEV, counts)
    counts = jnp.where(places == least_at, TILES_DEV // 4, counts)
    return counts.reshape(N_ROW, N_COL).astype(jnp.int32)


def plant(entries, key, smallest, largest):
    longest = entries.shape.index(max(entries.shape))
    spots = []
    for shift in (0, 1):
        where = [jax.random.randint(jax.random.fold_in(key, axis), (), 0, length) for axis, length in enumerate(entries.shape)]
        where[longest] = (where[longest] + shift) % entries.shape[longest]
        spots.append(tuple(where))
    return entries.at[spots[0]].set(smallest).at[spots[1]].set(largest)


def block_scale(key, shape, shards, low, high):
    level = 1.0
    for position, shards_of in shards:
        draws = jax.random.uniform(jax.random.fold_in(jax.random.fold_in(key, 6), position), (shards_of,), jnp.float32, low / len(shards), high / len(shards))
        level = level * jnp.repeat(jnp.exp(draws), shape[position] // shards_of).reshape((-1,) + (1,) * (len(shape) - 1 - position))
    return level


def gaussian(key, extent, spread, limit, cuts=(), held_as=jnp.bfloat16):
    values = spread * jax.random.normal(key, extent, jnp.float32)
    if cuts:
        values = values * block_scale(key, extent, cuts, -0.22, 0.18)
    return jnp.clip(values, -limit, limit).astype(held_as)


def setup_inputs(seed: int = 0) -> dict:
    keys = jax.random.split(jax.random.key(seed), 9)
    features = gaussian(keys[0], (NODES, F), 1.0, 6.0, ((0, 32),))
    weight = gaussian(keys[1], (F, F), F ** -0.5, 0.375)
    tile_coords = draw_tile_coords(jax.random.fold_in(keys[8], 71), 0)
    tile_live = draw_tile_live(jax.random.fold_in(keys[8], 71), 0)
    tile_edges = plant((jax.random.randint(keys[4], (N_ROW, N_COL, TILES_DEV, TILE, TILE), 0, 32) < 1).astype(jnp.int32), jax.random.fold_in(keys[4], 1), 0, 1)
    row_degree = plant(jax.random.randint(keys[5], (NODES,), 1, 65), jax.random.fold_in(keys[5], 1), 1, 64).astype(jnp.int32)
    col_degree = plant(jax.random.randint(keys[6], (NODES,), 1, 65), jax.random.fold_in(keys[6], 1), 1, 64).astype(jnp.int32)
    cotangent = gaussian(keys[7], (NODES, F), 1.0, 6.0, ((0, 32),))
    return dict(features=features, weight=weight, tile_coords=tile_coords, tile_live=tile_live, tile_edges=tile_edges, row_degree=row_degree, col_degree=col_degree, cotangent=cotangent)


def reference(features, weight, tile_coords, tile_live, tile_edges, row_degree, col_degree, cotangent):
    row_scale = lax.rsqrt(row_degree.astype(jnp.float32))
    col_scale = lax.rsqrt(col_degree.astype(jnp.float32))
    panel = (col_scale[:, None] * jnp.dot(features, weight, preferred_element_type=jnp.float32)).astype(jnp.bfloat16)
    panel_tiles = panel.reshape(NODES // TILE, TILE, F).astype(jnp.float32)
    slot_ids = jnp.arange(TILES_DEV, dtype=jnp.int32)

    def block_edges(device):
        row_block = device // N_COL
        col_block = device % N_COL
        coords = tile_coords[row_block, col_block]
        valid_slots = slot_ids < tile_live[row_block, col_block]
        local_edges = jnp.where(valid_slots[:, None, None], tile_edges[row_block, col_block], 0).astype(jnp.float32)
        rows_global = (row_block * ROW_TILES + coords[:, 0]).astype(jnp.int32)
        cols_global = (col_block * COL_TILES + coords[:, 1]).astype(jnp.int32)
        return (local_edges, rows_global, cols_global)

    def forward_step(totals, device):
        local_edges, rows_global, cols_global = block_edges(device)
        picked = panel_tiles[cols_global]
        products = jnp.einsum('sij,sjf->sif', local_edges, picked, precision=lax.Precision.HIGHEST)
        return (totals.at[rows_global].add(products), None)
    devices = jnp.arange(N_ROW * N_COL, dtype=jnp.int32)
    zeros_tiles = jnp.zeros((NODES // TILE, TILE, F), jnp.float32)
    summed, _ = lax.scan(forward_step, zeros_tiles, devices)
    aggregated = (row_scale[:, None] * summed.reshape(NODES, F)).astype(jnp.bfloat16)
    upstream = (row_scale[:, None] * cotangent.astype(jnp.float32)).astype(jnp.bfloat16)
    upstream_tiles = upstream.reshape(NODES // TILE, TILE, F).astype(jnp.float32)

    def backward_step(totals, device):
        local_edges, rows_global, cols_global = block_edges(device)
        picked = upstream_tiles[rows_global]
        products = jnp.einsum('sji,sjf->sif', local_edges, picked, precision=lax.Precision.HIGHEST)
        return (totals.at[cols_global].add(products), None)
    back_summed, _ = lax.scan(backward_step, zeros_tiles, devices)
    grad_panel = (col_scale[:, None] * back_summed.reshape(NODES, F)).astype(jnp.bfloat16)
    grad_features = jnp.dot(grad_panel, weight.T, preferred_element_type=jnp.float32).astype(jnp.bfloat16)
    grad_weight = jnp.dot(features.T, grad_panel, preferred_element_type=jnp.float32)
    return (aggregated, grad_features, grad_weight)
```

```python
import functools

import jax
import jax.numpy as jnp
from jax import lax
from jax.experimental import pallas as pl
from jax.experimental.pallas import tpu as pltpu
from jax.sharding import PartitionSpec as P

MESH = pl.DeviceIdType.MESH
CORES = 2
SLOW = 4
MB = 1024 * 1024


def greet(n_row, n_col, row, col):
    barrier = pltpu.get_barrier_semaphore()
    for k in range(1, n_row):
        peer = lax.rem(row + k, n_row)
        pl.semaphore_signal(barrier, inc=1, device_id=(peer, col), device_id_type=MESH)
    for k in range(1, n_col):
        peer = lax.rem(col + k, n_col)
        pl.semaphore_signal(barrier, inc=1, device_id=(row, peer), device_id_type=MESH)
    pl.semaphore_wait(barrier, n_row + n_col - 2)


def remote(src, dst, send, recv, target):
    return pltpu.make_async_remote_copy(
        src_ref=src,
        dst_ref=dst,
        send_sem=send,
        recv_sem=recv,
        device_id=target,
        device_id_type=MESH,
    )


def gather_kernel(
    n_row, n_col, feat, weight, col_scale, cot, row_scale, panel, upstream, p_send, p_recv, u_send, u_recv
):
    row = lax.axis_index("row")
    col = lax.axis_index("col")
    n_y = n_row // CORES
    n_fast = n_col // SLOW
    y, core = row // CORES, lax.rem(row, CORES)
    z, x = col // n_fast, lax.rem(col, n_fast)
    upstream[pl.ds(col, 1)] = (row_scale[...] * cot[...].astype(jnp.float32)).astype(jnp.bfloat16)[None]
    greet(n_row, n_col, row, col)

    def up_copy(slot, send, target):
        return remote(upstream.at[slot], upstream.at[slot], u_send.at[send], u_recv.at[slot], (row, target))

    def fan_fast(slot, base):
        for k in range(1, n_fast):
            up_copy(slot, base + k - 1, z * n_fast + lax.rem(x + k, n_fast)).start()

    def fan_fast_wait(slot, base):
        for k in range(1, n_fast):
            up_copy(slot, base + k - 1, z * n_fast + lax.rem(x + k, n_fast)).wait_send()

    per = n_fast
    up_ok, down_ok = z + 1 < SLOW, z >= 1

    @pl.when(up_ok)
    def _():
        up_copy(col, 0, col + n_fast).start()

    @pl.when(down_ok)
    def _():
        up_copy(col, 1, col - n_fast).start()

    fan_fast(col, 2)

    own = jnp.dot(feat[...], weight[...], preferred_element_type=jnp.float32)
    panel[pl.ds(row, 1)] = (col_scale[...] * own).astype(jnp.bfloat16)[None]

    def p_copy(slot, send, target):
        return remote(panel.at[slot], panel.at[slot], p_send.at[send], p_recv.at[slot], (target, col))

    other = y * CORES + (1 - core)
    for k in range(1, n_y):
        p_copy(row, k, lax.rem(y + k, n_y) * CORES + core).start()
    p_copy(row, 0, other).start()

    base = 2 + n_fast - 1
    for t in range(1, SLOW):
        for side in range(2):
            first = base + ((t - 1) * 2 + side) * per
            if side == 0:
                here, slot = z >= t, col - t * n_fast
                onward, target = up_ok, col + n_fast
            else:
                here, slot = z + t < SLOW, col + t * n_fast
                onward, target = down_ok, col - n_fast

            @pl.when(here)
            def _():
                up_copy(slot, first, col).wait_recv()

                @pl.when(onward)
                def _():
                    up_copy(slot, first, target).start()

                fan_fast(slot, first + 1)

        if t == 1:
            for k in range(1, n_y):
                slot = lax.rem(y + k, n_y) * CORES + core
                p_copy(slot, n_y - 1 + k, other).wait_recv()
                p_copy(slot, n_y - 1 + k, other).start()

    for k in range(n_y):
        slot = lax.rem(y + k, n_y) * CORES + (1 - core)
        p_copy(slot, 0, other).wait_recv()
    for k in range(1, n_fast):
        for t in range(SLOW):
            slot = t * n_fast + lax.rem(x + k, n_fast)
            up_copy(slot, 0, col).wait_recv()

    p_copy(row, 0, other).wait_send()
    for k in range(1, n_y):
        p_copy(row, k, other).wait_send()
        p_copy(row, n_y - 1 + k, other).wait_send()

    @pl.when(up_ok)
    def _():
        up_copy(col, 0, col).wait_send()

    @pl.when(down_ok)
    def _():
        up_copy(col, 1, col).wait_send()

    fan_fast_wait(col, 2)
    for t in range(1, SLOW):
        for side in range(2):
            first = base + ((t - 1) * 2 + side) * per
            if side == 0:
                here, onward = z >= t, up_ok
            else:
                here, onward = z + t < SLOW, down_ok

            @pl.when(here)
            def _():
                @pl.when(onward)
                def _():
                    up_copy(col, first, col).wait_send()

                fan_fast_wait(col, first + 1)


def tile_kernel(steps, group, coords, live, edges, panel, upstream, out, back, acc, back_acc):
    step = pl.program_id(0)
    row_tiles, col_tiles = out.shape[0], back.shape[0]

    @pl.when(step == 0)
    def _():
        acc[...] = jnp.zeros_like(acc)
        back_acc[...] = jnp.zeros_like(back_acc)

    unroll = 8 if group % 8 == 0 else 1

    def body(i, carry):
        for j in range(unroll):
            local = i * unroll + j
            slot = step * group + local
            r, c = coords[2 * slot], coords[2 * slot + 1]
            ok = slot < live[0]
            r_to = jnp.where(ok, r, row_tiles)
            c_to = jnp.where(ok, c, col_tiles)
            tile = edges[local].astype(jnp.float32).astype(jnp.bfloat16)
            acc[r_to] += jnp.dot(tile, panel[c], preferred_element_type=jnp.float32)
            back_acc[c_to] += lax.dot_general(
                tile, upstream[r], (((0,), (0,)), ((), ())), preferred_element_type=jnp.float32
            )
        return carry

    lax.fori_loop(0, group // unroll, body, 0)

    @pl.when(step == steps - 1)
    def _():
        out[...] = acc[:row_tiles].astype(jnp.bfloat16)
        back[...] = back_acc[:col_tiles].astype(jnp.bfloat16)


def scatter_kernel(
    n_row,
    n_col,
    part,
    back,
    feat,
    weight,
    row_scale,
    col_scale,
    out,
    grad_feat,
    grad_weight,
    x_buf,
    z_out,
    z_buf,
    c_buf,
    y_out,
    y_buf,
    w_out,
    w1_buf,
    q_out,
    w2_buf,
    q_all,
    w4_buf,
    x_send,
    x_recv,
    z_send,
    z_recv,
    c_send,
    c_recv,
    y_send,
    y_recv,
    w_send,
    w1_recv,
    w2_recv,
    w3_recv,
    w4_recv,
):
    row = lax.axis_index("row")
    col = lax.axis_index("col")
    n_y = n_row // CORES
    n_fast = n_col // SLOW
    y, core = row // CORES, lax.rem(row, CORES)
    z, x = col // n_fast, lax.rem(col, n_fast)
    f32, bf16 = jnp.float32, jnp.bfloat16
    other = y * CORES + (1 - core)
    greet(n_row, n_col, row, col)

    def c_copy(k):
        block = lax.rem(y + k, n_y) * CORES + (1 - core)
        return remote(back.at[block], c_buf.at[k], c_send.at[k], c_recv.at[k], (other, col))

    for k in reversed(range(n_y)):
        c_copy(k).start()

    def x_copy(t, k):
        to = lax.rem(x + k, n_fast)
        block = lax.rem(z + t, SLOW) * n_fast + to
        slot = t * (n_fast - 1) + k - 1
        return remote(
            part.at[block], x_buf.at[slot], x_send.at[slot], x_recv.at[slot], (row, z * n_fast + to)
        )

    order = (2, 3, 1, 0)
    for t in order:
        for k in range(1, n_fast):
            x_copy(t, k).start()

    def y_copy(k):
        return remote(
            y_out.at[k],
            y_buf.at[k],
            y_send.at[k],
            y_recv.at[k],
            (lax.rem(y + k, n_y) * CORES + core, col),
        )

    own_back = None
    for k in reversed(range(n_y)):
        c_copy(k).wait_recv()
        block = lax.rem(y + k, n_y) * CORES + core
        total = back[pl.ds(block, 1)][0].astype(f32) + c_buf[k].astype(f32)
        if k:
            y_out[k] = total.astype(bf16)
            y_copy(k).start()
        else:
            y_out[0] = total.astype(bf16)

    def z_copy(t):
        return remote(
            z_out.at[t],
            z_buf.at[t],
            z_send.at[t],
            z_recv.at[t],
            (row, lax.rem(z + t, SLOW) * n_fast + x),
        )

    def merge_x(t):
        block = lax.rem(z + t, SLOW) * n_fast + x
        total = part[pl.ds(block, 1)][0].astype(f32)
        for k in range(1, n_fast):
            x_copy(t, k).wait_recv()
            total = total + x_buf[t * (n_fast - 1) + k - 1].astype(f32)
        z_out[t] = total.astype(bf16)
        if t:
            z_copy(t).start()

    merge_x(order[0])

    total = y_out[0].astype(f32)
    for k in range(1, n_y):
        y_copy(k).wait_recv()
        total = total + y_buf[k].astype(f32)
    grad_panel = (col_scale[...] * total).astype(bf16)
    terms = lax.dot_general(feat[...], grad_panel, (((0,), (0,)), ((), ())), preferred_element_type=f32)
    quarter = terms.shape[0] // n_row
    piece = quarter // n_col
    for r in range(n_row):
        w_out[r] = terms[r * quarter : (r + 1) * quarter]

    def w1_copy(k):
        to = lax.rem(row + k, n_row)
        return remote(w_out.at[to], w1_buf.at[k], w_send.at[k], w1_recv.at[k], (to, col))

    for k in range(1, n_row):
        w1_copy(k).start()
    grad_feat[...] = lax.dot_general(
        grad_panel, weight[...], (((1,), (1,)), ((), ())), preferred_element_type=f32
    ).astype(bf16)

    merge_x(order[1])

    total = w_out[pl.ds(row, 1)][0]
    for k in range(1, n_row):
        w1_copy(k).wait_recv()
        total = total + w1_buf[k]
    for j in range(n_col):
        q_out[j] = total[j * piece : (j + 1) * piece]

    def w2_copy(k):
        to = lax.rem(col + k, n_col)
        return remote(q_out.at[to], w2_buf.at[k], w_send.at[n_row + k], w2_recv.at[k], (row, to))

    for k in range(1, n_col):
        w2_copy(k).start()

    merge_x(order[2])

    total = q_out[pl.ds(col, 1)][0]
    for k in range(1, n_col):
        w2_copy(k).wait_recv()
        total = total + w2_buf[k]
    q_all[pl.ds(col, 1)] = total[None]

    def w3_copy(k):
        to = lax.rem(col + k, n_col)
        return remote(
            q_all.at[col], q_all.at[col], w_send.at[n_row + n_col + k], w3_recv.at[k], (row, to)
        )

    for k in range(1, n_col):
        w3_copy(k).start()

    merge_x(order[3])

    for k in range(1, n_col):
        w3_copy(k).wait_recv()
    for j in range(n_col):
        w4_buf[pl.ds(row, 1), j * piece : (j + 1) * piece] = q_all[j][None]

    def w4_copy(k):
        to = lax.rem(row + k, n_row)
        return remote(
            w4_buf.at[row], w4_buf.at[row], w_send.at[n_row + 2 * n_col + k], w4_recv.at[k], (to, col)
        )

    for k in range(1, n_row):
        w4_copy(k).start()

    total = z_out[0].astype(f32)
    for t in order[:3]:
        z_copy(t).wait_recv()
        total = total + z_buf[t].astype(f32)
    out[...] = (row_scale[...] * total).astype(bf16)

    for k in range(1, n_row):
        w4_copy(k).wait_recv()
    for r in range(n_row):
        grad_weight[r * quarter : (r + 1) * quarter] = w4_buf[r]

    for k in range(n_y):
        c_copy(k).wait_send()
        if k:
            y_copy(k).wait_send()
    for t in range(SLOW):
        for k in range(1, n_fast):
            x_copy(t, k).wait_send()
        if t:
            z_copy(t).wait_send()
    for k in range(1, n_row):
        w1_copy(k).wait_send()
        w4_copy(k).wait_send()
    for k in range(1, n_col):
        w2_copy(k).wait_send()
        w3_copy(k).wait_send()


def vmem(n):
    return [pl.BlockSpec(memory_space=pltpu.VMEM)] * n


def shards(
    n_row, n_col, features, weight, tile_coords, tile_live, tile_edges, row_degree, col_degree, cotangent
):
    f32, bf16 = jnp.float32, jnp.bfloat16
    dma, shape = pltpu.SemaphoreType.DMA, jax.ShapeDtypeStruct
    tile = tile_edges.shape[-1]
    slots = tile_edges.shape[2]
    nodes, width = features.shape
    n_y, n_fast = n_row // CORES, n_col // SLOW
    row_scale = lax.rsqrt(row_degree.astype(f32))[:, None]
    col_scale = lax.rsqrt(col_degree.astype(f32))[:, None]

    panel, upstream = pl.pallas_call(
        functools.partial(gather_kernel, n_row, n_col),
        out_shape=(shape((n_row, nodes, width), bf16), shape((n_col, nodes, width), bf16)),
        in_specs=vmem(5),
        out_specs=tuple(vmem(2)),
        scratch_shapes=[
            dma((2 * n_y,)),
            dma((n_row,)),
            dma((2 + n_fast - 1 + 2 * (SLOW - 1) * n_fast,)),
            dma((n_col,)),
        ],
        compiler_params=pltpu.CompilerParams(
            collective_id=0, has_side_effects=True, vmem_limit_bytes=40 * MB
        ),
        name="gather",
    )(features, weight, col_scale, cotangent, row_scale)

    col_tiles = n_row * nodes // tile
    row_tiles = n_col * nodes // tile
    group = max(g for g in range(1, 25) if slots % g == 0)
    steps = slots // group
    part, back = pl.pallas_call(
        functools.partial(tile_kernel, steps, group),
        out_shape=(shape((row_tiles, tile, width), bf16), shape((col_tiles, tile, width), bf16)),
        grid_spec=pltpu.PrefetchScalarGridSpec(
            num_scalar_prefetch=2,
            grid=(steps,),
            in_specs=[
                pl.BlockSpec((group, tile, tile), lambda i, *_: (i, 0, 0)),
                pl.BlockSpec(memory_space=pltpu.VMEM),
                pl.BlockSpec(memory_space=pltpu.VMEM),
            ],
            out_specs=(
                pl.BlockSpec((row_tiles, tile, width), lambda i, *_: (0, 0, 0)),
                pl.BlockSpec((col_tiles, tile, width), lambda i, *_: (0, 0, 0)),
            ),
            scratch_shapes=[
                pltpu.VMEM((row_tiles + 1, tile, width), f32),
                pltpu.VMEM((col_tiles + 1, tile, width), f32),
            ],
        ),
        compiler_params=pltpu.CompilerParams(vmem_limit_bytes=48 * MB),
        name="tiles",
    )(
        tile_coords.reshape(-1),
        tile_live.reshape(-1),
        tile_edges[0, 0],
        panel.reshape(col_tiles, tile, width),
        upstream.reshape(row_tiles, tile, width),
    )

    quarter = width // n_row
    piece = quarter // n_col
    block = (nodes, width)
    return pl.pallas_call(
        functools.partial(scatter_kernel, n_row, n_col),
        out_shape=(shape(block, bf16), shape(block, bf16), shape((width, width), f32)),
        in_specs=vmem(6),
        out_specs=tuple(vmem(3)),
        scratch_shapes=[
            pltpu.VMEM((SLOW * (n_fast - 1),) + block, bf16),
            pltpu.VMEM((SLOW,) + block, bf16),
            pltpu.VMEM((SLOW,) + block, bf16),
            pltpu.VMEM((n_y,) + block, bf16),
            pltpu.VMEM((n_y,) + block, bf16),
            pltpu.VMEM((n_y,) + block, bf16),
            pltpu.VMEM((n_row, quarter, width), f32),
            pltpu.VMEM((n_row, quarter, width), f32),
            pltpu.VMEM((n_col, piece, width), f32),
            pltpu.VMEM((n_col, piece, width), f32),
            pltpu.VMEM((n_col, piece, width), f32),
            pltpu.VMEM((n_row, quarter, width), f32),
            dma((SLOW * (n_fast - 1),)),
            dma((SLOW * (n_fast - 1),)),
            dma((SLOW,)),
            dma((SLOW,)),
            dma((n_y,)),
            dma((n_y,)),
            dma((n_y,)),
            dma((n_y,)),
            dma((2 * n_row + 2 * n_col,)),
            dma((n_row,)),
            dma((n_col,)),
            dma((n_col,)),
            dma((n_row,)),
        ],
        compiler_params=pltpu.CompilerParams(
            collective_id=1, has_side_effects=True, vmem_limit_bytes=56 * MB
        ),
        name="scatter",
    )(
        part.reshape((n_col,) + block),
        back.reshape((n_row,) + block),
        features,
        weight,
        row_scale,
        col_scale,
    )


def solution(mesh):
    in_specs = (
        P(("col", "row"), None),
        P(),
        P("row", "col", None, None),
        P("row", "col"),
        P("row", "col", None, None, None),
        P(("row", "col")),
        P(("col", "row")),
        P(("row", "col"), None),
    )
    out_specs = (P(("row", "col"), None), P(("col", "row"), None), P())
    body = functools.partial(shards, mesh.shape["row"], mesh.shape["col"])
    return jax.shard_map(body, mesh=mesh, in_specs=in_specs, out_specs=out_specs, check_vma=False)
```

```python
import functools

import jax
import jax.numpy as jnp
from jax import lax
from jax.experimental import pallas as pl
from jax.experimental.pallas import tpu as pltpu
from jax.sharding import PartitionSpec as P

MESH = pl.DeviceIdType.MESH
CORES = 2
SLOW = 4
MB = 1024 * 1024


def greet(n_row, n_col, row, col):
    barrier = pltpu.get_barrier_semaphore()
    for k in range(1, n_row):
        peer = lax.rem(row + k, n_row)
        pl.semaphore_signal(barrier, inc=1, device_id=(peer, col), device_id_type=MESH)
    for k in range(1, n_col):
        peer = lax.rem(col + k, n_col)
        pl.semaphore_signal(barrier, inc=1, device_id=(row, peer), device_id_type=MESH)
    pl.semaphore_wait(barrier, n_row + n_col - 2)


def remote(src, dst, send, recv, target):
    return pltpu.make_async_remote_copy(
        src_ref=src,
        dst_ref=dst,
        send_sem=send,
        recv_sem=recv,
        device_id=target,
        device_id_type=MESH,
    )


def table_kernel(row_tiles, col_tiles, coords, coords_t, live, tab):
    slots, lanes = coords.shape[0], tab.shape[1]
    count = live[0]
    s_col = lax.broadcasted_iota(jnp.int32, (slots, 1), 0)
    s_row = lax.broadcasted_iota(jnp.int32, (1, lanes), 1)
    place = lax.broadcasted_iota(jnp.int32, (slots, lanes), 1)
    for half, tiles in ((0, row_tiles), (1, col_tiles)):
        key_col = jnp.where(s_col < count, coords[:, half : half + 1], tiles)
        key_row = jnp.where(s_row < count, coords_t[half : half + 1, :], tiles)
        same = (key_row == key_col) & (s_row < s_col)
        earlier = jnp.sum(same.astype(jnp.int32), axis=1, keepdims=True)
        below = jnp.sum((key_row < key_col).astype(jnp.int32), axis=1, keepdims=True)
        chosen = ((earlier + below) == place).astype(jnp.int32)
        source = coords[:, 1 - half : 2 - half]
        follows = (earlier > 0).astype(jnp.int32)
        upto = jnp.sum((key_col <= place).astype(jnp.int32), axis=0, keepdims=True)
        here = jnp.sum((key_col == place).astype(jnp.int32), axis=0, keepdims=True)
        tab[4 * half : 4 * half + 1, :] = jnp.sum(chosen * s_col, axis=0, keepdims=True)
        tab[4 * half + 1 : 4 * half + 2, :] = jnp.sum(chosen * source, axis=0, keepdims=True)
        tab[4 * half + 2 : 4 * half + 3, :] = jnp.sum(chosen * follows, axis=0, keepdims=True)
        tab[4 * half + 3 : 4 * half + 4, :] = jnp.where(here > 0, upto - 1, slots)


def layer_kernel(
    n_row,
    n_col,
    tab,
    feat,
    weight,
    col_scale,
    cot,
    row_scale,
    edges_hbm,
    out,
    grad_feat,
    grad_weight,
    edges,
    panel,
    upstream,
    acc,
    sums,
    part,
    back,
    x_buf,
    z_out,
    z_buf,
    c_buf,
    y_out,
    y_buf,
    w_out,
    w1_buf,
    q_out,
    w2_buf,
    q_all,
    w4_buf,
    e_sem,
    p_send,
    p_recv,
    u_send,
    u_recv,
    x_send,
    x_recv,
    z_send,
    z_recv,
    c_send,
    c_recv,
    y_send,
    y_recv,
    w_send,
    w1_recv,
    w2_recv,
    w3_recv,
    w4_recv,
):
    row = lax.axis_index("row")
    col = lax.axis_index("col")
    n_y = n_row // CORES
    n_fast = n_col // SLOW
    y, core = row // CORES, lax.rem(row, CORES)
    z, x = col // n_fast, lax.rem(col, n_fast)
    f32, bf16 = jnp.float32, jnp.bfloat16
    other = y * CORES + (1 - core)
    slots, tile = edges.shape[0], edges.shape[1]
    tiles_dev = panel.shape[1]
    nodes, width = feat.shape
    block_shape = (tiles_dev, tile, width)

    load_edges = pltpu.make_async_copy(edges_hbm, edges, e_sem)
    load_edges.start()
    own = (row_scale[...] * cot[...].astype(f32)).astype(bf16)
    upstream[pl.ds(col, 1)] = own.reshape((1,) + block_shape)
    greet(n_row, n_col, row, col)

    def up_copy(slot, send, target):
        return remote(upstream.at[slot], upstream.at[slot], u_send.at[send], u_recv.at[slot], (row, target))

    def fan_fast(slot, base):
        for k in range(1, n_fast):
            up_copy(slot, base + k - 1, z * n_fast + lax.rem(x + k, n_fast)).start()

    def fan_fast_wait(slot, base):
        for k in range(1, n_fast):
            up_copy(slot, base + k - 1, z * n_fast + lax.rem(x + k, n_fast)).wait_send()

    up_ok, down_ok = z + 1 < SLOW, z >= 1
    up_base = 2 + n_fast - 1

    @pl.when(up_ok)
    def _():
        up_copy(col, 0, col + n_fast).start()

    @pl.when(down_ok)
    def _():
        up_copy(col, 1, col - n_fast).start()

    fan_fast(col, 2)

    def pass_on(t):
        for side in range(2):
            first = up_base + ((t - 1) * 2 + side) * n_fast
            if side == 0:
                here, slot = z >= t, col - t * n_fast
                onward, target = up_ok, col + n_fast
            else:
                here, slot = z + t < SLOW, col + t * n_fast
                onward, target = down_ok, col - n_fast

            @pl.when(here)
            def _():
                up_copy(slot, first, col).wait_recv()

                @pl.when(onward)
                def _():
                    up_copy(slot, first, target).start()

                fan_fast(slot, first + 1)

    own = jnp.dot(feat[...], weight[...], preferred_element_type=f32)
    panel[pl.ds(row, 1)] = (col_scale[...] * own).astype(bf16).reshape((1,) + block_shape)

    def p_copy(slot, send, target):
        return remote(panel.at[slot], panel.at[slot], p_send.at[send], p_recv.at[slot], (target, col))

    for k in range(1, n_y):
        p_copy(row, k, lax.rem(y + k, n_y) * CORES + core).start()
    p_copy(row, 0, other).start()
    acc[...] = jnp.zeros_like(acc)
    sums[slots] = jnp.zeros((tile, width), bf16)
    for k in range(1, n_y):
        slot = lax.rem(y + k, n_y) * CORES + core
        p_copy(slot, n_y - 1 + k, other).wait_recv()
        p_copy(slot, n_y - 1 + k, other).start()
    pass_on(1)
    for k in range(n_y):
        slot = lax.rem(y + k, n_y) * CORES + (1 - core)
        p_copy(slot, 0, other).wait_recv()
    load_edges.wait()

    unroll = 8 if slots % 16 == 0 else 1

    def products(base, source, flipped, lo, hi):
        def body(i, carry):
            for j in range(unroll):
                n = lo + i * unroll + j
                pick, src = tab[base, n], tab[base + 1, n]
                keep = tab[base + 2, n].astype(f32)
                mat = edges[pick].astype(f32).astype(bf16)
                vals = source[lax.div(src, tiles_dev), lax.rem(src, tiles_dev)]
                dims = (((0,), (0,)), ((), ())) if flipped else (((1,), (0,)), ((), ()))
                total = acc[...] * keep + lax.dot_general(mat, vals, dims, preferred_element_type=f32)
                acc[...] = total
                sums[n] = total.astype(bf16)
            return carry

        lax.fori_loop(0, (hi - lo) // unroll, body, 0)

    half = slots // 2
    products(0, panel, False, 0, half)
    pass_on(2)
    products(0, panel, False, half, slots)
    for block in range(n_col):
        for j in range(tiles_dev):
            part[block, j] = sums[tab[3, block * tiles_dev + j]]

    def x_copy(t, k):
        to = lax.rem(x + k, n_fast)
        block = lax.rem(z + t, SLOW) * n_fast + to
        slot = t * (n_fast - 1) + k - 1
        return remote(
            part.at[block], x_buf.at[slot], x_send.at[slot], x_recv.at[slot], (row, z * n_fast + to)
        )

    order = (2, 3, 1, 0)

    def start_x(i):
        if i >= 2:
            for k in range(1, n_fast):
                x_copy(order[i - 2], k).wait_send()
        for k in range(1, n_fast):
            x_copy(order[i], k).start()

    for t in range(3, SLOW):
        pass_on(t)
    start_x(0)
    start_x(1)

    def z_copy(t):
        return remote(
            z_out.at[t],
            z_buf.at[t],
            z_send.at[t],
            z_recv.at[t],
            (row, lax.rem(z + t, SLOW) * n_fast + x),
        )

    def merge_x(i):
        t = order[i]
        block = lax.rem(z + t, SLOW) * n_fast + x
        total = part[pl.ds(block, 1)][0].astype(f32)
        for k in range(1, n_fast):
            x_copy(t, k).wait_recv()
            total = total + x_buf[t * (n_fast - 1) + k - 1].astype(f32)
        z_out[t] = total.astype(bf16)
        if t:
            z_copy(t).start()

    for k in range(1, n_fast):
        for t in range(SLOW):
            slot = t * n_fast + lax.rem(x + k, n_fast)
            up_copy(slot, 0, col).wait_recv()
    products(4, upstream, True, 0, half)
    merge_x(0)
    start_x(2)
    products(4, upstream, True, half, slots)
    for block in range(n_row):
        for j in range(tiles_dev):
            back[block, j] = sums[tab[7, block * tiles_dev + j]]

    def c_copy(k):
        block = lax.rem(y + k, n_y) * CORES + (1 - core)
        return remote(back.at[block], c_buf.at[k], c_send.at[k], c_recv.at[k], (other, col))

    for k in reversed(range(n_y)):
        c_copy(k).start()

    def y_copy(k):
        return remote(
            y_out.at[k],
            y_buf.at[k],
            y_send.at[k],
            y_recv.at[k],
            (lax.rem(y + k, n_y) * CORES + core, col),
        )

    for k in reversed(range(n_y)):
        c_copy(k).wait_recv()
        block = lax.rem(y + k, n_y) * CORES + core
        total = back[pl.ds(block, 1)][0].astype(f32) + c_buf[k].astype(f32)
        y_out[k] = total.astype(bf16)
        if k:
            y_copy(k).start()

    merge_x(1)
    start_x(3)

    total = y_out[0].astype(f32)
    for k in range(1, n_y):
        y_copy(k).wait_recv()
        total = total + y_buf[k].astype(f32)
    grad_panel = (col_scale[...] * total.reshape((nodes, width))).astype(bf16)
    terms = lax.dot_general(feat[...], grad_panel, (((0,), (0,)), ((), ())), preferred_element_type=f32)
    quarter = width // n_row
    piece = quarter // n_col
    for r in range(n_row):
        w_out[r] = terms[r * quarter : (r + 1) * quarter]

    def w1_copy(k):
        to = lax.rem(row + k, n_row)
        return remote(w_out.at[to], w1_buf.at[k], w_send.at[k], w1_recv.at[k], (to, col))

    for k in range(1, n_row):
        w1_copy(k).start()
    grad_feat[...] = lax.dot_general(
        grad_panel, weight[...], (((1,), (1,)), ((), ())), preferred_element_type=f32
    ).astype(bf16)

    merge_x(2)

    total = w_out[pl.ds(row, 1)][0]
    for k in range(1, n_row):
        w1_copy(k).wait_recv()
        total = total + w1_buf[k]
    for j in range(n_col):
        q_out[j] = total[j * piece : (j + 1) * piece]

    def w2_copy(k):
        to = lax.rem(col + k, n_col)
        return remote(q_out.at[to], w2_buf.at[k], w_send.at[n_row + k], w2_recv.at[k], (row, to))

    for k in range(1, n_col):
        w2_copy(k).start()

    merge_x(3)

    total = q_out[pl.ds(col, 1)][0]
    for k in range(1, n_col):
        w2_copy(k).wait_recv()
        total = total + w2_buf[k]
    q_all[pl.ds(col, 1)] = total[None]

    def w3_copy(k):
        to = lax.rem(col + k, n_col)
        return remote(
            q_all.at[col], q_all.at[col], w_send.at[n_row + n_col + k], w3_recv.at[k], (row, to)
        )

    for k in range(1, n_col):
        w3_copy(k).start()

    total = z_out[0].astype(f32)
    for t in order[:3]:
        z_copy(t).wait_recv()
        total = total + z_buf[t].astype(f32)
    out[...] = (row_scale[...] * total.reshape((nodes, width))).astype(bf16)

    for k in range(1, n_col):
        w3_copy(k).wait_recv()
    for j in range(n_col):
        w4_buf[pl.ds(row, 1), j * piece : (j + 1) * piece] = q_all[j][None]

    def w4_copy(k):
        to = lax.rem(row + k, n_row)
        return remote(
            w4_buf.at[row], w4_buf.at[row], w_send.at[n_row + 2 * n_col + k], w4_recv.at[k], (to, col)
        )

    for k in range(1, n_row):
        w4_copy(k).start()

    p_copy(row, 0, other).wait_send()
    for k in range(1, n_y):
        p_copy(row, k, other).wait_send()
        p_copy(row, n_y - 1 + k, other).wait_send()

    @pl.when(up_ok)
    def _():
        up_copy(col, 0, col).wait_send()

    @pl.when(down_ok)
    def _():
        up_copy(col, 1, col).wait_send()

    fan_fast_wait(col, 2)
    for t in range(1, SLOW):
        for side in range(2):
            first = up_base + ((t - 1) * 2 + side) * n_fast
            if side == 0:
                here, onward = z >= t, up_ok
            else:
                here, onward = z + t < SLOW, down_ok

            @pl.when(here)
            def _():
                @pl.when(onward)
                def _():
                    up_copy(col, first, col).wait_send()

                fan_fast_wait(col, first + 1)

    for k in range(n_y):
        c_copy(k).wait_send()
        if k:
            y_copy(k).wait_send()
    for t in order[2:]:
        for k in range(1, n_fast):
            x_copy(t, k).wait_send()
    for t in order[:3]:
        z_copy(t).wait_send()
    for k in range(1, n_row):
        w1_copy(k).wait_send()
    for k in range(1, n_col):
        w2_copy(k).wait_send()
        w3_copy(k).wait_send()

    for k in range(1, n_row):
        w4_copy(k).wait_recv()
    for r in range(n_row):
        grad_weight[r * quarter : (r + 1) * quarter] = w4_buf[r]
    for k in range(1, n_row):
        w4_copy(k).wait_send()


def vmem(n):
    return [pl.BlockSpec(memory_space=pltpu.VMEM)] * n


def shards(
    n_row, n_col, features, weight, tile_coords, tile_live, tile_edges, row_degree, col_degree, cotangent
):
    f32, bf16 = jnp.float32, jnp.bfloat16
    dma, shape = pltpu.SemaphoreType.DMA, jax.ShapeDtypeStruct
    tile = tile_edges.shape[-1]
    slots = tile_edges.shape[2]
    nodes, width = features.shape
    n_y, n_fast = n_row // CORES, n_col // SLOW
    row_scale = lax.rsqrt(row_degree.astype(f32))[:, None]
    col_scale = lax.rsqrt(col_degree.astype(f32))[:, None]
    tiles_dev = nodes // tile
    col_tiles = n_row * tiles_dev
    row_tiles = n_col * tiles_dev
    lanes = pl.cdiv(max(slots, row_tiles), 128) * 128
    coords = tile_coords[0, 0]
    tab = pl.pallas_call(
        functools.partial(table_kernel, row_tiles, col_tiles),
        out_shape=shape((8, lanes), jnp.int32),
        in_specs=vmem(2) + [pl.BlockSpec(memory_space=pltpu.SMEM)],
        out_specs=pl.BlockSpec(memory_space=pltpu.VMEM),
        name="tables",
    )(coords, jnp.pad(coords.T, ((0, 0), (0, lanes - slots))), tile_live.reshape(-1))

    quarter = width // n_row
    piece = quarter // n_col
    block = (tiles_dev, tile, width)
    return pl.pallas_call(
        functools.partial(layer_kernel, n_row, n_col),
        out_shape=(
            shape((nodes, width), bf16),
            shape((nodes, width), bf16),
            shape((width, width), f32),
        ),
        in_specs=[pl.BlockSpec(memory_space=pltpu.SMEM)]
        + vmem(5)
        + [pl.BlockSpec(memory_space=pl.ANY)],
        out_specs=tuple(vmem(3)),
        scratch_shapes=[
            pltpu.VMEM((slots, tile, tile), jnp.int32),
            pltpu.VMEM((n_row,) + block, bf16),
            pltpu.VMEM((n_col,) + block, bf16),
            pltpu.VMEM((tile, width), f32),
            pltpu.VMEM((slots + 1, tile, width), bf16),
            pltpu.VMEM((n_col,) + block, bf16),
            pltpu.VMEM((n_row,) + block, bf16),
            pltpu.VMEM((SLOW * (n_fast - 1),) + block, bf16),
            pltpu.VMEM((SLOW,) + block, bf16),
            pltpu.VMEM((SLOW,) + block, bf16),
            pltpu.VMEM((n_y,) + block, bf16),
            pltpu.VMEM((n_y,) + block, bf16),
            pltpu.VMEM((n_y,) + block, bf16),
            pltpu.VMEM((n_row, quarter, width), f32),
            pltpu.VMEM((n_row, quarter, width), f32),
            pltpu.VMEM((n_col, piece, width), f32),
            pltpu.VMEM((n_col, piece, width), f32),
            pltpu.VMEM((n_col, piece, width), f32),
            pltpu.VMEM((n_row, quarter, width), f32),
            dma(()),
            dma((2 * n_y,)),
            dma((n_row,)),
            dma((2 + n_fast - 1 + 2 * (SLOW - 1) * n_fast,)),
            dma((n_col,)),
            dma((SLOW * (n_fast - 1),)),
            dma((SLOW * (n_fast - 1),)),
            dma((SLOW,)),
            dma((SLOW,)),
            dma((n_y,)),
            dma((n_y,)),
            dma((n_y,)),
            dma((n_y,)),
            dma((2 * n_row + 2 * n_col,)),
            dma((n_row,)),
            dma((n_col,)),
            dma((n_col,)),
            dma((n_row,)),
        ],
        compiler_params=pltpu.CompilerParams(
            collective_id=0, has_side_effects=True, vmem_limit_bytes=56 * MB
        ),
        name="layer",
    )(tab, features, weight, col_scale, cotangent, row_scale, tile_edges[0, 0])


def solution(mesh):
    in_specs = (
        P(("col", "row"), None),
        P(),
        P("row", "col", None, None),
        P("row", "col"),
        P("row", "col", None, None, None),
        P(("row", "col")),
        P(("col", "row")),
        P(("row", "col"), None),
    )
    out_specs = (P(("row", "col"), None), P(("col", "row"), None), P())
    body = functools.partial(shards, mesh.shape["row"], mesh.shape["col"])
    return jax.shard_map(body, mesh=mesh, in_specs=in_specs, out_specs=out_specs, check_vma=False)
```

```python
import functools

import jax
import jax.numpy as jnp
from jax import lax
from jax.experimental import pallas as pl
from jax.experimental.pallas import tpu as pltpu
from jax.sharding import PartitionSpec as P

MESH = pl.DeviceIdType.MESH
CORES = 2
SLOW = 4
MB = 1024 * 1024


def greet(n_row, n_col, row, col):
    barrier = pltpu.get_barrier_semaphore()
    for k in range(1, n_row):
        peer = lax.rem(row + k, n_row)
        pl.semaphore_signal(barrier, inc=1, device_id=(peer, col), device_id_type=MESH)
    for k in range(1, n_col):
        peer = lax.rem(col + k, n_col)
        pl.semaphore_signal(barrier, inc=1, device_id=(row, peer), device_id_type=MESH)
    pl.semaphore_wait(barrier, n_row + n_col - 2)


def remote(src, dst, send, recv, target):
    return pltpu.make_async_remote_copy(
        src_ref=src,
        dst_ref=dst,
        send_sem=send,
        recv_sem=recv,
        device_id=target,
        device_id_type=MESH,
    )


def fill_tables(row_tiles, col_tiles, packed, turned, count, slots, tab):
    lanes = tab.shape[1]
    coords, coords_t = turned[:slots], packed
    s_col = lax.broadcasted_iota(jnp.int32, (slots, 1), 0)
    s_row = lax.broadcasted_iota(jnp.int32, (1, lanes), 1)
    place = lax.broadcasted_iota(jnp.int32, (slots, lanes), 1)
    for half, tiles in ((0, row_tiles), (1, col_tiles)):
        key_col = jnp.where(s_col < count, coords[:, half : half + 1], tiles)
        key_row = jnp.where(s_row < count, coords_t[half : half + 1, :], tiles)
        same = (key_row == key_col) & (s_row < s_col)
        earlier = jnp.sum(same.astype(jnp.int32), axis=1, keepdims=True)
        below = jnp.sum((key_row < key_col).astype(jnp.int32), axis=1, keepdims=True)
        chosen = ((earlier + below) == place).astype(jnp.int32)
        source = coords[:, 1 - half : 2 - half]
        follows = (earlier > 0).astype(jnp.int32)
        upto = jnp.sum((key_col <= place).astype(jnp.int32), axis=0, keepdims=True)
        here = jnp.sum((key_col == place).astype(jnp.int32), axis=0, keepdims=True)
        tab[4 * half : 4 * half + 1, :] = jnp.sum(chosen * s_col, axis=0, keepdims=True)
        tab[4 * half + 1 : 4 * half + 2, :] = jnp.sum(chosen * source, axis=0, keepdims=True)
        tab[4 * half + 2 : 4 * half + 3, :] = jnp.sum(chosen * follows, axis=0, keepdims=True)
        tab[4 * half + 3 : 4 * half + 4, :] = jnp.where(here > 0, upto - 1, slots)


def layer_kernel(
    n_row,
    n_col,
    live,
    packed,
    feat,
    weight,
    cot,
    edges_hbm,
    out,
    grad_feat,
    grad_weight,
    edges,
    turned_edges,
    tab_vmem,
    tab,
    row_scale,
    col_scale,
    panel,
    upstream,
    acc,
    sums,
    part,
    back,
    x_buf,
    z_out,
    z_buf,
    c_buf,
    y_out,
    y_buf,
    w_out,
    w1_buf,
    q_out,
    w2_buf,
    q_all,
    w4_buf,
    e_sem,
    t_sem,
    p_send,
    p_recv,
    u_send,
    u_recv,
    x_send,
    x_recv,
    z_send,
    z_recv,
    c_send,
    c_recv,
    y_send,
    y_recv,
    w_send,
    w1_recv,
    w2_recv,
    w3_recv,
    w4_recv,
):
    row = lax.axis_index("row")
    col = lax.axis_index("col")
    n_y = n_row // CORES
    n_fast = n_col // SLOW
    y, core = row // CORES, lax.rem(row, CORES)
    z, x = col // n_fast, lax.rem(col, n_fast)
    f32, bf16 = jnp.float32, jnp.bfloat16
    other = y * CORES + (1 - core)
    slots, tile = edges.shape[0], edges.shape[1]
    tiles_dev = panel.shape[1]
    nodes, width = feat.shape
    block_shape = (tiles_dev, tile, width)

    load_edges = pltpu.make_async_copy(edges_hbm, edges, e_sem)
    load_edges.start()
    table = packed[...]
    turned = jnp.transpose(table)
    lanes = table.shape[1]
    for h in range(nodes // lanes):
        at = slice(h * lanes, (h + 1) * lanes)
        row_scale[at, :] = lax.rsqrt(turned[:, 2 + h : 3 + h].astype(f32))
        first = 2 + nodes // lanes + h
        col_scale[at, :] = lax.rsqrt(turned[:, first : first + 1].astype(f32))
    own = (row_scale[...] * cot[...].astype(f32)).astype(bf16)
    upstream[pl.ds(col, 1)] = own.reshape((1,) + block_shape)
    greet(n_row, n_col, row, col)

    def up_copy(slot, send, target):
        return remote(upstream.at[slot], upstream.at[slot], u_send.at[send], u_recv.at[slot], (row, target))

    def fan_fast(slot, base):
        for k in range(1, n_fast):
            up_copy(slot, base + k - 1, z * n_fast + lax.rem(x + k, n_fast)).start()

    def fan_fast_wait(slot, base):
        for k in range(1, n_fast):
            up_copy(slot, base + k - 1, z * n_fast + lax.rem(x + k, n_fast)).wait_send()

    up_ok, down_ok = z + 1 < SLOW, z >= 1
    up_base = 2 + n_fast - 1

    @pl.when(up_ok)
    def _():
        up_copy(col, 0, col + n_fast).start()

    @pl.when(down_ok)
    def _():
        up_copy(col, 1, col - n_fast).start()

    fan_fast(col, 2)

    def pass_on(t):
        for side in range(2):
            first = up_base + ((t - 1) * 2 + side) * n_fast
            if side == 0:
                here, slot = z >= t, col - t * n_fast
                onward, target = up_ok, col + n_fast
            else:
                here, slot = z + t < SLOW, col + t * n_fast
                onward, target = down_ok, col - n_fast

            @pl.when(here)
            def _():
                up_copy(slot, first, col).wait_recv()

                @pl.when(onward)
                def _():
                    up_copy(slot, first, target).start()

                fan_fast(slot, first + 1)

    own = jnp.dot(feat[...], weight[...], preferred_element_type=f32)
    panel[pl.ds(row, 1)] = (col_scale[...] * own).astype(bf16).reshape((1,) + block_shape)

    def p_copy(slot, send, target):
        return remote(panel.at[slot], panel.at[slot], p_send.at[send], p_recv.at[slot], (target, col))

    for k in range(1, n_y):
        p_copy(row, k, lax.rem(y + k, n_y) * CORES + core).start()
    p_copy(row, 0, other).start()
    fill_tables(n_col * tiles_dev, n_row * tiles_dev, table, turned, live[0], slots, tab_vmem)
    load_tab = pltpu.make_async_copy(tab_vmem, tab, t_sem)
    load_tab.start()
    acc[...] = jnp.zeros_like(acc)
    sums[slots] = jnp.zeros((tile, width), bf16)
    for k in range(1, n_y):
        slot = lax.rem(y + k, n_y) * CORES + core
        p_copy(slot, n_y - 1 + k, other).wait_recv()
        p_copy(slot, n_y - 1 + k, other).start()
    pass_on(1)
    for k in range(n_y):
        slot = lax.rem(y + k, n_y) * CORES + (1 - core)
        p_copy(slot, 0, other).wait_recv()
    load_edges.wait()
    load_tab.wait()

    unroll = 8 if slots % 16 == 0 else 1

    def products(base, source, flipped, lo, hi):
        def body(i, carry):
            for j in range(unroll):
                n = lo + i * unroll + j
                pick, src = tab[base, n], tab[base + 1, n]
                keep = tab[base + 2, n].astype(f32)
                mat = turned_edges[pick] if flipped else edges[pick].astype(f32).astype(bf16)
                vals = source[lax.div(src, tiles_dev), lax.rem(src, tiles_dev)]
                total = acc[...] * keep + jnp.dot(mat, vals, preferred_element_type=f32)
                acc[...] = total
                sums[n] = total.astype(bf16)
            return carry

        lax.fori_loop(0, (hi - lo) // unroll, body, 0)

    half = slots // 2
    products(0, panel, False, 0, half)
    pass_on(2)
    products(0, panel, False, half, slots)
    for block in range(n_col):
        for j in range(tiles_dev):
            part[block, j] = sums[tab[3, block * tiles_dev + j]]

    def x_copy(t, k):
        to = lax.rem(x + k, n_fast)
        block = lax.rem(z + t, SLOW) * n_fast + to
        slot = t * (n_fast - 1) + k - 1
        return remote(
            part.at[block], x_buf.at[slot], x_send.at[slot], x_recv.at[slot], (row, z * n_fast + to)
        )

    order = (2, 3, 1, 0)

    def start_x(i):
        if i >= 2:
            for k in range(1, n_fast):
                x_copy(order[i - 2], k).wait_send()
        for k in range(1, n_fast):
            x_copy(order[i], k).start()

    for t in range(3, SLOW):
        pass_on(t)

    def turn(i, carry):
        for j in range(unroll):
            n = i * unroll + j
            turned_edges[n] = jnp.transpose(edges[n].astype(f32)).astype(bf16)
        return carry

    lax.fori_loop(0, slots // unroll, turn, 0)

    def z_copy(t):
        return remote(
            z_out.at[t],
            z_buf.at[t],
            z_send.at[t],
            z_recv.at[t],
            (row, lax.rem(z + t, SLOW) * n_fast + x),
        )

    def merge_x(i):
        t = order[i]
        block = lax.rem(z + t, SLOW) * n_fast + x
        total = part[pl.ds(block, 1)][0].astype(f32)
        for k in range(1, n_fast):
            x_copy(t, k).wait_recv()
            total = total + x_buf[t * (n_fast - 1) + k - 1].astype(f32)
        z_out[t] = total.astype(bf16)
        if t:
            z_copy(t).start()

    for k in range(1, n_fast):
        for t in range(SLOW):
            slot = t * n_fast + lax.rem(x + k, n_fast)
            up_copy(slot, 0, col).wait_recv()
    start_x(0)
    start_x(1)
    products(4, upstream, True, 0, half)
    merge_x(0)
    start_x(2)
    products(4, upstream, True, half, slots)
    for block in range(n_row):
        for j in range(tiles_dev):
            back[block, j] = sums[tab[7, block * tiles_dev + j]]

    def c_copy(k):
        block = lax.rem(y + k, n_y) * CORES + (1 - core)
        return remote(back.at[block], c_buf.at[k], c_send.at[k], c_recv.at[k], (other, col))

    for k in reversed(range(n_y)):
        c_copy(k).start()

    def y_copy(k):
        return remote(
            y_out.at[k],
            y_buf.at[k],
            y_send.at[k],
            y_recv.at[k],
            (lax.rem(y + k, n_y) * CORES + core, col),
        )

    for k in reversed(range(n_y)):
        c_copy(k).wait_recv()
        block = lax.rem(y + k, n_y) * CORES + core
        total = back[pl.ds(block, 1)][0].astype(f32) + c_buf[k].astype(f32)
        y_out[k] = total.astype(bf16)
        if k:
            y_copy(k).start()

    merge_x(1)
    start_x(3)

    total = y_out[0].astype(f32)
    for k in range(1, n_y):
        y_copy(k).wait_recv()
        total = total + y_buf[k].astype(f32)
    grad_panel = (col_scale[...] * total.reshape((nodes, width))).astype(bf16)
    terms = lax.dot_general(feat[...], grad_panel, (((0,), (0,)), ((), ())), preferred_element_type=f32)
    quarter = width // n_row
    piece = quarter // n_col
    for r in range(n_row):
        w_out[r] = terms[r * quarter : (r + 1) * quarter]

    def w1_copy(k):
        to = lax.rem(row + k, n_row)
        return remote(w_out.at[to], w1_buf.at[k], w_send.at[k], w1_recv.at[k], (to, col))

    for k in range(1, n_row):
        w1_copy(k).start()
    grad_feat[...] = lax.dot_general(
        grad_panel, weight[...], (((1,), (1,)), ((), ())), preferred_element_type=f32
    ).astype(bf16)

    merge_x(2)

    total = w_out[pl.ds(row, 1)][0]
    for k in range(1, n_row):
        w1_copy(k).wait_recv()
        total = total + w1_buf[k]
    for j in range(n_col):
        q_out[j] = total[j * piece : (j + 1) * piece]

    def w2_copy(k):
        to = lax.rem(col + k, n_col)
        return remote(q_out.at[to], w2_buf.at[k], w_send.at[n_row + k], w2_recv.at[k], (row, to))

    for k in range(1, n_col):
        w2_copy(k).start()

    merge_x(3)

    total = q_out[pl.ds(col, 1)][0]
    for k in range(1, n_col):
        w2_copy(k).wait_recv()
        total = total + w2_buf[k]
    q_all[pl.ds(col, 1)] = total[None]

    def w3_copy(k):
        to = lax.rem(col + k, n_col)
        return remote(
            q_all.at[col], q_all.at[col], w_send.at[n_row + n_col + k], w3_recv.at[k], (row, to)
        )

    for k in range(1, n_col):
        w3_copy(k).start()

    total = z_out[0].astype(f32)
    for t in order[:3]:
        z_copy(t).wait_recv()
        total = total + z_buf[t].astype(f32)
    out[...] = (row_scale[...] * total.reshape((nodes, width))).astype(bf16)

    for k in range(1, n_col):
        w3_copy(k).wait_recv()
    for j in range(n_col):
        w4_buf[pl.ds(row, 1), j * piece : (j + 1) * piece] = q_all[j][None]

    def w4_copy(k):
        to = lax.rem(row + k, n_row)
        return remote(
            w4_buf.at[row], w4_buf.at[row], w_send.at[n_row + 2 * n_col + k], w4_recv.at[k], (to, col)
        )

    for k in range(1, n_row):
        w4_copy(k).start()

    p_copy(row, 0, other).wait_send()
    for k in range(1, n_y):
        p_copy(row, k, other).wait_send()
        p_copy(row, n_y - 1 + k, other).wait_send()

    @pl.when(up_ok)
    def _():
        up_copy(col, 0, col).wait_send()

    @pl.when(down_ok)
    def _():
        up_copy(col, 1, col).wait_send()

    fan_fast_wait(col, 2)
    for t in range(1, SLOW):
        for side in range(2):
            first = up_base + ((t - 1) * 2 + side) * n_fast
            if side == 0:
                here, onward = z >= t, up_ok
            else:
                here, onward = z + t < SLOW, down_ok

            @pl.when(here)
            def _():
                @pl.when(onward)
                def _():
                    up_copy(col, first, col).wait_send()

                fan_fast_wait(col, first + 1)

    for k in range(n_y):
        c_copy(k).wait_send()
        if k:
            y_copy(k).wait_send()
    for t in order[2:]:
        for k in range(1, n_fast):
            x_copy(t, k).wait_send()
    for t in order[:3]:
        z_copy(t).wait_send()
    for k in range(1, n_row):
        w1_copy(k).wait_send()
    for k in range(1, n_col):
        w2_copy(k).wait_send()
        w3_copy(k).wait_send()

    for k in range(1, n_row):
        w4_copy(k).wait_recv()
    for r in range(n_row):
        grad_weight[r * quarter : (r + 1) * quarter] = w4_buf[r]
    for k in range(1, n_row):
        w4_copy(k).wait_send()


def hand_over_kernel(a, b, c, a_out, b_out, c_out, sems):
    pairs = ((a, a_out), (b, b_out), (c, c_out))
    copies = [pltpu.make_async_copy(src, dst, sems.at[i]) for i, (src, dst) in enumerate(pairs)]
    for copy in copies:
        copy.start()
    for copy in copies:
        copy.wait()


def vmem(n):
    return [pl.BlockSpec(memory_space=pltpu.VMEM)] * n


def shards(
    n_row, n_col, features, weight, tile_coords, tile_live, tile_edges, row_degree, col_degree, cotangent
):
    f32, bf16 = jnp.float32, jnp.bfloat16
    dma, shape = pltpu.SemaphoreType.DMA, jax.ShapeDtypeStruct
    tile = tile_edges.shape[-1]
    slots = tile_edges.shape[2]
    nodes, width = features.shape
    n_y, n_fast = n_row // CORES, n_col // SLOW
    tiles_dev = nodes // tile
    row_tiles = n_col * tiles_dev
    lanes = pl.cdiv(max(slots, row_tiles), 128) * 128
    coords = jnp.pad(tile_coords[0, 0].T, ((0, 0), (0, lanes - slots)))
    degrees = [row_degree.reshape(-1, lanes), col_degree.reshape(-1, lanes)]
    used = 2 + 2 * degrees[0].shape[0]
    packed = jnp.pad(jnp.concatenate([coords] + degrees), ((0, -used % 8), (0, 0)))

    quarter = width // n_row
    piece = quarter // n_col
    block = (tiles_dev, tile, width)
    results = pl.pallas_call(
        functools.partial(layer_kernel, n_row, n_col),
        out_shape=(
            shape((nodes, width), bf16),
            shape((nodes, width), bf16),
            shape((width, width), f32),
        ),
        in_specs=[pl.BlockSpec(memory_space=pltpu.SMEM)]
        + vmem(4)
        + [pl.BlockSpec(memory_space=pl.ANY)],
        out_specs=tuple(vmem(3)),
        scratch_shapes=[
            pltpu.VMEM((slots, tile, tile), jnp.int32),
            pltpu.VMEM((slots, tile, tile), bf16),
            pltpu.VMEM((8, lanes), jnp.int32),
            pltpu.SMEM((8, lanes), jnp.int32),
            pltpu.VMEM((nodes, 1), f32),
            pltpu.VMEM((nodes, 1), f32),
            pltpu.VMEM((n_row,) + block, bf16),
            pltpu.VMEM((n_col,) + block, bf16),
            pltpu.VMEM((tile, width), f32),
            pltpu.VMEM((slots + 1, tile, width), bf16),
            pltpu.VMEM((n_col,) + block, bf16),
            pltpu.VMEM((n_row,) + block, bf16),
            pltpu.VMEM((SLOW * (n_fast - 1),) + block, bf16),
            pltpu.VMEM((SLOW,) + block, bf16),
            pltpu.VMEM((SLOW,) + block, bf16),
            pltpu.VMEM((n_y,) + block, bf16),
            pltpu.VMEM((n_y,) + block, bf16),
            pltpu.VMEM((n_y,) + block, bf16),
            pltpu.VMEM((n_row, quarter, width), f32),
            pltpu.VMEM((n_row, quarter, width), f32),
            pltpu.VMEM((n_col, piece, width), f32),
            pltpu.VMEM((n_col, piece, width), f32),
            pltpu.VMEM((n_col, piece, width), f32),
            pltpu.VMEM((n_row, quarter, width), f32),
            dma(()),
            dma(()),
            dma((2 * n_y,)),
            dma((n_row,)),
            dma((2 + n_fast - 1 + 2 * (SLOW - 1) * n_fast,)),
            dma((n_col,)),
            dma((SLOW * (n_fast - 1),)),
            dma((SLOW * (n_fast - 1),)),
            dma((SLOW,)),
            dma((SLOW,)),
            dma((n_y,)),
            dma((n_y,)),
            dma((n_y,)),
            dma((n_y,)),
            dma((2 * n_row + 2 * n_col,)),
            dma((n_row,)),
            dma((n_col,)),
            dma((n_col,)),
            dma((n_row,)),
        ],
        compiler_params=pltpu.CompilerParams(
            collective_id=0, has_side_effects=True, vmem_limit_bytes=56 * MB
        ),
        name="layer",
    )(tile_live.reshape(-1), packed, features, weight, cotangent, tile_edges[0, 0])
    return pl.pallas_call(
        hand_over_kernel,
        out_shape=tuple(shape(r.shape, r.dtype) for r in results),
        in_specs=[pl.BlockSpec(memory_space=pl.ANY)] * 3,
        out_specs=tuple([pl.BlockSpec(memory_space=pl.ANY)] * 3),
        scratch_shapes=[dma((3,))],
        compiler_params=pltpu.CompilerParams(vmem_limit_bytes=60 * MB),
        name="hand_over",
    )(*results)


def solution(mesh):
    in_specs = (
        P(("col", "row"), None),
        P(),
        P("row", "col", None, None),
        P("row", "col"),
        P("row", "col", None, None, None),
        P(("row", "col")),
        P(("col", "row")),
        P(("row", "col"), None),
    )
    out_specs = (P(("row", "col"), None), P(("col", "row"), None), P())
    body = functools.partial(shards, mesh.shape["row"], mesh.shape["col"])
    return jax.shard_map(body, mesh=mesh, in_specs=in_specs, out_specs=out_specs, check_vma=False)
```

```python
import functools

import jax
import jax.numpy as jnp
from jax import lax
from jax.experimental import pallas as pl
from jax.experimental.pallas import tpu as pltpu
from jax.sharding import PartitionSpec as P

MESH = pl.DeviceIdType.MESH
CORES = 2
SLOW = 4
MB = 1024 * 1024


def greet(n_row, n_col, row, col):
    barrier = pltpu.get_barrier_semaphore()
    for k in range(1, n_row):
        peer = lax.rem(row + k, n_row)
        pl.semaphore_signal(barrier, inc=1, device_id=(peer, col), device_id_type=MESH)
    for k in range(1, n_col):
        peer = lax.rem(col + k, n_col)
        pl.semaphore_signal(barrier, inc=1, device_id=(row, peer), device_id_type=MESH)
    pl.semaphore_wait(barrier, n_row + n_col - 2)


def remote(src, dst, send, recv, target):
    return pltpu.make_async_remote_copy(
        src_ref=src,
        dst_ref=dst,
        send_sem=send,
        recv_sem=recv,
        device_id=target,
        device_id_type=MESH,
    )


def fill_tables(row_tiles, col_tiles, packed, turned, count, slots, tab):
    lanes = tab.shape[1]
    coords, coords_t = turned[:slots], packed
    s_col = lax.broadcasted_iota(jnp.int32, (slots, 1), 0)
    s_row = lax.broadcasted_iota(jnp.int32, (1, lanes), 1)
    place = lax.broadcasted_iota(jnp.int32, (slots, lanes), 1)
    for half, tiles in ((0, row_tiles), (1, col_tiles)):
        key_col = jnp.where(s_col < count, coords[:, half : half + 1], tiles)
        key_row = jnp.where(s_row < count, coords_t[half : half + 1, :], tiles)
        same = (key_row == key_col) & (s_row < s_col)
        earlier = jnp.sum(same.astype(jnp.int32), axis=1, keepdims=True)
        below = jnp.sum((key_row < key_col).astype(jnp.int32), axis=1, keepdims=True)
        chosen = ((earlier + below) == place).astype(jnp.int32)
        source = coords[:, 1 - half : 2 - half]
        follows = (earlier > 0).astype(jnp.int32)
        upto = jnp.sum((key_col <= place).astype(jnp.int32), axis=0, keepdims=True)
        here = jnp.sum((key_col == place).astype(jnp.int32), axis=0, keepdims=True)
        tab[4 * half : 4 * half + 1, :] = jnp.sum(chosen * s_col, axis=0, keepdims=True)
        tab[4 * half + 1 : 4 * half + 2, :] = jnp.sum(chosen * source, axis=0, keepdims=True)
        tab[4 * half + 2 : 4 * half + 3, :] = jnp.sum(chosen * follows, axis=0, keepdims=True)
        tab[4 * half + 3 : 4 * half + 4, :] = jnp.where(here > 0, upto - 1, slots)


def layer_kernel(
    n_row,
    n_col,
    live,
    coords,
    row_degree,
    col_degree,
    feat,
    weight,
    cot,
    edges_hbm,
    out,
    grad_feat,
    grad_weight,
    edges,
    turned_edges,
    packed,
    tab_vmem,
    tab,
    row_scale,
    col_scale,
    panel,
    turned_feat,
    upstream,
    acc,
    sums,
    part,
    back,
    x_buf,
    z_out,
    z_buf,
    c_buf,
    y_out,
    y_buf,
    w_out,
    w1_buf,
    q_out,
    w2_buf,
    q_all,
    w4_buf,
    e_sem,
    t_sem,
    p_send,
    p_recv,
    f_send,
    f_recv,
    u_send,
    u_recv,
    x_send,
    x_recv,
    z_send,
    z_recv,
    c_send,
    c_recv,
    y_send,
    y_recv,
    w_send,
    w1_recv,
    w2_recv,
    w3_recv,
    w4_recv,
):
    row = lax.axis_index("row")
    col = lax.axis_index("col")
    n_y = n_row // CORES
    n_fast = n_col // SLOW
    y, core = row // CORES, lax.rem(row, CORES)
    z, x = col // n_fast, lax.rem(col, n_fast)
    f32, bf16 = jnp.float32, jnp.bfloat16
    other = y * CORES + (1 - core)
    slots, tile = edges.shape[0], edges.shape[1]
    tiles_dev = panel.shape[1]
    nodes, width = feat.shape
    block_shape = (tiles_dev, tile, width)

    load_edges = pltpu.make_async_copy(edges_hbm, edges, e_sem)
    load_edges.start()
    lanes = row_degree.shape[1]
    parts = nodes // lanes
    packed[...] = jnp.zeros_like(packed)
    packed[0:2, :slots] = coords[...]
    packed[2 : 2 + parts] = row_degree[...]
    packed[2 + parts : 2 + 2 * parts] = col_degree[...]
    table = packed[...]
    turned = jnp.transpose(table)
    for h in range(parts):
        at = slice(h * lanes, (h + 1) * lanes)
        row_scale[at, :] = lax.rsqrt(turned[:, 2 + h : 3 + h].astype(f32))
        first = 2 + parts + h
        col_scale[at, :] = lax.rsqrt(turned[:, first : first + 1].astype(f32))
    own = (row_scale[...] * cot[...].astype(f32)).astype(bf16)
    upstream[pl.ds(col, 1)] = own.reshape((1,) + block_shape)
    greet(n_row, n_col, row, col)

    def up_copy(slot, send, target):
        return remote(upstream.at[slot], upstream.at[slot], u_send.at[send], u_recv.at[slot], (row, target))

    def fan_fast(slot, base):
        for k in range(1, n_fast):
            up_copy(slot, base + k - 1, z * n_fast + lax.rem(x + k, n_fast)).start()

    def fan_fast_wait(slot, base):
        for k in range(1, n_fast):
            up_copy(slot, base + k - 1, z * n_fast + lax.rem(x + k, n_fast)).wait_send()

    up_ok, down_ok = z + 1 < SLOW, z >= 1
    up_base = 2 + n_fast - 1

    @pl.when(up_ok)
    def _():
        up_copy(col, 0, col + n_fast).start()

    @pl.when(down_ok)
    def _():
        up_copy(col, 1, col - n_fast).start()

    fan_fast(col, 2)

    def pass_on(t):
        for side in range(2):
            first = up_base + ((t - 1) * 2 + side) * n_fast
            if side == 0:
                here, slot = z >= t, col - t * n_fast
                onward, target = up_ok, col + n_fast
            else:
                here, slot = z + t < SLOW, col + t * n_fast
                onward, target = down_ok, col - n_fast

            @pl.when(here)
            def _():
                up_copy(slot, first, col).wait_recv()

                @pl.when(onward)
                def _():
                    up_copy(slot, first, target).start()

                fan_fast(slot, first + 1)

    own = jnp.dot(feat[...], weight[...], preferred_element_type=f32)
    panel[pl.ds(row, 1)] = (col_scale[...] * own).astype(bf16).reshape((1,) + block_shape)

    def p_copy(slot, send, target):
        return remote(panel.at[slot], panel.at[slot], p_send.at[send], p_recv.at[slot], (target, col))

    for k in range(1, n_y):
        p_copy(row, k, lax.rem(y + k, n_y) * CORES + core).start()
    p_copy(row, 0, other).start()

    scaled = jnp.transpose(col_scale[...] * feat[...].astype(f32))
    turned_feat[pl.ds(row, 1)] = scaled.astype(bf16)[None]

    def f_copy(slot, send, target):
        return remote(
            turned_feat.at[slot], turned_feat.at[slot], f_send.at[send], f_recv.at[slot], (target, col)
        )

    for k in range(1, n_y):
        f_copy(row, k, lax.rem(y + k, n_y) * CORES + core).start()
    f_copy(row, 0, other).start()
    fill_tables(n_col * tiles_dev, n_row * tiles_dev, table, turned, live[0], slots, tab_vmem)
    load_tab = pltpu.make_async_copy(tab_vmem, tab, t_sem)
    load_tab.start()
    acc[...] = jnp.zeros_like(acc)
    sums[slots] = jnp.zeros((tile, width), bf16)
    for k in range(1, n_y):
        slot = lax.rem(y + k, n_y) * CORES + core
        p_copy(slot, n_y - 1 + k, other).wait_recv()
        p_copy(slot, n_y - 1 + k, other).start()
    pass_on(1)
    for k in range(n_y):
        slot = lax.rem(y + k, n_y) * CORES + (1 - core)
        p_copy(slot, 0, other).wait_recv()
    load_edges.wait()
    load_tab.wait()

    unroll = 8 if slots % 16 == 0 else 1

    def products(base, source, flipped, lo, hi):
        def body(i, carry):
            for j in range(unroll):
                n = lo + i * unroll + j
                pick, src = tab[base, n], tab[base + 1, n]
                keep = tab[base + 2, n].astype(f32)
                mat = turned_edges[pick] if flipped else edges[pick].astype(f32).astype(bf16)
                vals = source[lax.div(src, tiles_dev), lax.rem(src, tiles_dev)]
                total = acc[...] * keep + jnp.dot(mat, vals, preferred_element_type=f32)
                acc[...] = total
                sums[n] = total.astype(bf16)
            return carry

        lax.fori_loop(0, (hi - lo) // unroll, body, 0)

    half = slots // 2
    products(0, panel, False, 0, half)
    pass_on(2)
    for k in range(1, n_y):
        slot = lax.rem(y + k, n_y) * CORES + core
        f_copy(slot, n_y - 1 + k, other).wait_recv()
        f_copy(slot, n_y - 1 + k, other).start()
    products(0, panel, False, half, slots)
    for block in range(n_col):
        for j in range(tiles_dev):
            part[block, j] = sums[tab[3, block * tiles_dev + j]]

    def x_copy(t, k):
        to = lax.rem(x + k, n_fast)
        block = lax.rem(z + t, SLOW) * n_fast + to
        slot = t * (n_fast - 1) + k - 1
        return remote(
            part.at[block], x_buf.at[slot], x_send.at[slot], x_recv.at[slot], (row, z * n_fast + to)
        )

    order = (2, 3, 1, 0)

    def start_x(i):
        if i >= 2:
            for k in range(1, n_fast):
                x_copy(order[i - 2], k).wait_send()
        for k in range(1, n_fast):
            x_copy(order[i], k).start()

    for t in range(3, SLOW):
        pass_on(t)

    def turn(i, carry):
        for j in range(unroll):
            n = i * unroll + j
            turned_edges[n] = jnp.transpose(edges[n].astype(f32)).astype(bf16)
        return carry

    lax.fori_loop(0, slots // unroll, turn, 0)

    def z_copy(t):
        return remote(
            z_out.at[t],
            z_buf.at[t],
            z_send.at[t],
            z_recv.at[t],
            (row, lax.rem(z + t, SLOW) * n_fast + x),
        )

    def merge_x(i):
        t = order[i]
        block = lax.rem(z + t, SLOW) * n_fast + x
        total = part[pl.ds(block, 1)][0].astype(f32)
        for k in range(1, n_fast):
            x_copy(t, k).wait_recv()
            total = total + x_buf[t * (n_fast - 1) + k - 1].astype(f32)
        z_out[t] = total.astype(bf16)
        if t:
            z_copy(t).start()

    for k in range(1, n_fast):
        for t in range(SLOW):
            slot = t * n_fast + lax.rem(x + k, n_fast)
            up_copy(slot, 0, col).wait_recv()
    start_x(0)
    products(4, upstream, True, 0, half)
    start_x(1)
    products(4, upstream, True, half, slots)
    for block in range(n_row):
        for j in range(tiles_dev):
            back[block, j] = sums[tab[7, block * tiles_dev + j]]

    def c_copy(k):
        block = lax.rem(y + k, n_y) * CORES + (1 - core)
        return remote(back.at[block], c_buf.at[k], c_send.at[k], c_recv.at[k], (other, col))

    for k in reversed(range(n_y)):
        c_copy(k).start()

    for k in range(n_y):
        slot = lax.rem(y + k, n_y) * CORES + (1 - core)
        f_copy(slot, 0, other).wait_recv()
    quarter = width // n_row
    piece = quarter // n_col
    terms = jnp.zeros((width, width), f32)
    for block in range(n_row):
        terms = terms + jnp.dot(
            turned_feat[block], back[block].reshape((nodes, width)), preferred_element_type=f32
        )
    for r in range(n_row):
        w_out[r] = terms[r * quarter : (r + 1) * quarter]

    def w1_copy(k):
        to = lax.rem(row + k, n_row)
        return remote(w_out.at[to], w1_buf.at[k], w_send.at[k], w1_recv.at[k], (to, col))

    for k in range(1, n_row):
        w1_copy(k).start()

    def y_copy(k):
        return remote(
            y_out.at[k],
            y_buf.at[k],
            y_send.at[k],
            y_recv.at[k],
            (lax.rem(y + k, n_y) * CORES + core, col),
        )

    for k in reversed(range(n_y)):
        c_copy(k).wait_recv()
        block = lax.rem(y + k, n_y) * CORES + core
        total = back[pl.ds(block, 1)][0].astype(f32) + c_buf[k].astype(f32)
        y_out[k] = total.astype(bf16)
        if k:
            y_copy(k).start()

    merge_x(0)
    start_x(2)

    total = w_out[pl.ds(row, 1)][0]
    for k in range(1, n_row):
        w1_copy(k).wait_recv()
        total = total + w1_buf[k]
    for j in range(n_col):
        q_out[j] = total[j * piece : (j + 1) * piece]

    def w2_copy(k):
        to = lax.rem(col + k, n_col)
        return remote(q_out.at[to], w2_buf.at[k], w_send.at[n_row + k], w2_recv.at[k], (row, to))

    for k in range(1, n_col):
        w2_copy(k).start()

    merge_x(1)
    start_x(3)

    total = y_out[0].astype(f32)
    for k in range(1, n_y):
        y_copy(k).wait_recv()
        total = total + y_buf[k].astype(f32)
    grad_panel = (col_scale[...] * total.reshape((nodes, width))).astype(bf16)
    grad_feat[...] = lax.dot_general(
        grad_panel, weight[...], (((1,), (1,)), ((), ())), preferred_element_type=f32
    ).astype(bf16)

    total = q_out[pl.ds(col, 1)][0]
    for k in range(1, n_col):
        w2_copy(k).wait_recv()
        total = total + w2_buf[k]
    q_all[pl.ds(col, 1)] = total[None]

    def w3_copy(k):
        to = lax.rem(col + k, n_col)
        return remote(
            q_all.at[col], q_all.at[col], w_send.at[n_row + n_col + k], w3_recv.at[k], (row, to)
        )

    for k in range(1, n_col):
        w3_copy(k).start()

    merge_x(2)

    for k in range(1, n_col):
        w3_copy(k).wait_recv()
    for j in range(n_col):
        w4_buf[pl.ds(row, 1), j * piece : (j + 1) * piece] = q_all[j][None]

    def w4_copy(k):
        to = lax.rem(row + k, n_row)
        return remote(
            w4_buf.at[row], w4_buf.at[row], w_send.at[n_row + 2 * n_col + k], w4_recv.at[k], (to, col)
        )

    for k in range(1, n_row):
        w4_copy(k).start()

    merge_x(3)

    total = z_out[0].astype(f32)
    for t in order[:3]:
        z_copy(t).wait_recv()
        total = total + z_buf[t].astype(f32)
    out[...] = (row_scale[...] * total.reshape((nodes, width))).astype(bf16)

    f_copy(row, 0, other).wait_send()
    p_copy(row, 0, other).wait_send()
    for k in range(1, n_y):
        f_copy(row, k, other).wait_send()
        f_copy(row, n_y - 1 + k, other).wait_send()
        p_copy(row, k, other).wait_send()
        p_copy(row, n_y - 1 + k, other).wait_send()

    @pl.when(up_ok)
    def _():
        up_copy(col, 0, col).wait_send()

    @pl.when(down_ok)
    def _():
        up_copy(col, 1, col).wait_send()

    fan_fast_wait(col, 2)
    for t in range(1, SLOW):
        for side in range(2):
            first = up_base + ((t - 1) * 2 + side) * n_fast
            if side == 0:
                here, onward = z >= t, up_ok
            else:
                here, onward = z + t < SLOW, down_ok

            @pl.when(here)
            def _():
                @pl.when(onward)
                def _():
                    up_copy(col, first, col).wait_send()

                fan_fast_wait(col, first + 1)

    for k in range(n_y):
        c_copy(k).wait_send()
        if k:
            y_copy(k).wait_send()
    for t in order[2:]:
        for k in range(1, n_fast):
            x_copy(t, k).wait_send()
    for t in order[:3]:
        z_copy(t).wait_send()
    for k in range(1, n_row):
        w1_copy(k).wait_send()
    for k in range(1, n_col):
        w2_copy(k).wait_send()
        w3_copy(k).wait_send()

    for k in range(1, n_row):
        w4_copy(k).wait_recv()
    for r in range(n_row):
        grad_weight[r * quarter : (r + 1) * quarter] = w4_buf[r]
    for k in range(1, n_row):
        w4_copy(k).wait_send()


def hand_over_kernel(a, b, c, a_out, b_out, c_out):
    a_out[...] = a[...]
    b_out[...] = b[...]
    c_out[...] = c[...]


def vmem(n):
    return [pl.BlockSpec(memory_space=pltpu.VMEM)] * n


def shards(
    n_row, n_col, features, weight, tile_coords, tile_live, tile_edges, row_degree, col_degree, cotangent
):
    f32, bf16 = jnp.float32, jnp.bfloat16
    dma, shape = pltpu.SemaphoreType.DMA, jax.ShapeDtypeStruct
    tile = tile_edges.shape[-1]
    slots = tile_edges.shape[2]
    nodes, width = features.shape
    n_y, n_fast = n_row // CORES, n_col // SLOW
    tiles_dev = nodes // tile
    row_tiles = n_col * tiles_dev
    lanes = pl.cdiv(max(slots, row_tiles), 128) * 128
    coords = tile_coords[0, 0].T
    degrees = (row_degree.reshape(-1, lanes), col_degree.reshape(-1, lanes))

    quarter = width // n_row
    piece = quarter // n_col
    block = (tiles_dev, tile, width)
    results = pl.pallas_call(
        functools.partial(layer_kernel, n_row, n_col),
        out_shape=(
            shape((nodes, width), bf16),
            shape((nodes, width), bf16),
            shape((width, width), f32),
        ),
        in_specs=[pl.BlockSpec(memory_space=pltpu.SMEM)]
        + vmem(6)
        + [pl.BlockSpec(memory_space=pl.ANY)],
        out_specs=tuple(vmem(3)),
        scratch_shapes=[
            pltpu.VMEM((slots, tile, tile), jnp.int32),
            pltpu.VMEM((slots, tile, tile), bf16),
            pltpu.VMEM((8, lanes), jnp.int32),
            pltpu.VMEM((8, lanes), jnp.int32),
            pltpu.SMEM((8, lanes), jnp.int32),
            pltpu.VMEM((nodes, 1), f32),
            pltpu.VMEM((nodes, 1), f32),
            pltpu.VMEM((n_row,) + block, bf16),
            pltpu.VMEM((n_row, width, nodes), bf16),
            pltpu.VMEM((n_col,) + block, bf16),
            pltpu.VMEM((tile, width), f32),
            pltpu.VMEM((slots + 1, tile, width), bf16),
            pltpu.VMEM((n_col,) + block, bf16),
            pltpu.VMEM((n_row,) + block, bf16),
            pltpu.VMEM((SLOW * (n_fast - 1),) + block, bf16),
            pltpu.VMEM((SLOW,) + block, bf16),
            pltpu.VMEM((SLOW,) + block, bf16),
            pltpu.VMEM((n_y,) + block, bf16),
            pltpu.VMEM((n_y,) + block, bf16),
            pltpu.VMEM((n_y,) + block, bf16),
            pltpu.VMEM((n_row, quarter, width), f32),
            pltpu.VMEM((n_row, quarter, width), f32),
            pltpu.VMEM((n_col, piece, width), f32),
            pltpu.VMEM((n_col, piece, width), f32),
            pltpu.VMEM((n_col, piece, width), f32),
            pltpu.VMEM((n_row, quarter, width), f32),
            dma(()),
            dma(()),
            dma((2 * n_y,)),
            dma((n_row,)),
            dma((2 * n_y,)),
            dma((n_row,)),
            dma((2 + n_fast - 1 + 2 * (SLOW - 1) * n_fast,)),
            dma((n_col,)),
            dma((SLOW * (n_fast - 1),)),
            dma((SLOW * (n_fast - 1),)),
            dma((SLOW,)),
            dma((SLOW,)),
            dma((n_y,)),
            dma((n_y,)),
            dma((n_y,)),
            dma((n_y,)),
            dma((2 * n_row + 2 * n_col,)),
            dma((n_row,)),
            dma((n_col,)),
            dma((n_col,)),
            dma((n_row,)),
        ],
        compiler_params=pltpu.CompilerParams(
            collective_id=0, has_side_effects=True, vmem_limit_bytes=56 * MB
        ),
        name="layer",
    )(tile_live.reshape(-1), coords, *degrees, features, weight, cotangent, tile_edges[0, 0])
    return pl.pallas_call(
        hand_over_kernel,
        out_shape=tuple(shape(r.shape, r.dtype) for r in results),
        in_specs=vmem(3),
        out_specs=tuple(vmem(3)),
        compiler_params=pltpu.CompilerParams(vmem_limit_bytes=60 * MB),
        name="hand_over",
    )(*results)


def solution(mesh):
    in_specs = (
        P(("col", "row"), None),
        P(),
        P("row", "col", None, None),
        P("row", "col"),
        P("row", "col", None, None, None),
        P(("row", "col")),
        P(("col", "row")),
        P(("row", "col"), None),
    )
    out_specs = (P(("row", "col"), None), P(("col", "row"), None), P())
    body = functools.partial(shards, mesh.shape["row"], mesh.shape["col"])
    return jax.shard_map(body, mesh=mesh, in_specs=in_specs, out_specs=out_specs, check_vma=False)
```

```python
import functools

import jax
import jax.numpy as jnp
from jax import lax
from jax.experimental import pallas as pl
from jax.experimental.pallas import tpu as pltpu
from jax.sharding import PartitionSpec as P

MESH = pl.DeviceIdType.MESH
CORES = 2
SLOW = 4
JOIN = 4
MB = 1024 * 1024


def greet(n_row, n_col, row, col):
    barrier = pltpu.get_barrier_semaphore()
    for k in range(1, n_row):
        peer = lax.rem(row + k, n_row)
        pl.semaphore_signal(barrier, inc=1, device_id=(peer, col), device_id_type=MESH)
    for k in range(1, n_col):
        peer = lax.rem(col + k, n_col)
        pl.semaphore_signal(barrier, inc=1, device_id=(row, peer), device_id_type=MESH)
    pl.semaphore_wait(barrier, n_row + n_col - 2)


def remote(src, dst, send, recv, target):
    return pltpu.make_async_remote_copy(
        src_ref=src,
        dst_ref=dst,
        send_sem=send,
        recv_sem=recv,
        device_id=target,
        device_id_type=MESH,
    )


def groups_of(slots, tiles):
    return (slots + (JOIN - 1) * tiles) // JOIN


def fill_tables(row_tiles, col_tiles, packed, turned, count, slots, tab):
    lanes, wide = packed.shape[1], tab.shape[1]
    s_col = lax.broadcasted_iota(jnp.int32, (slots, 1), 0)
    s_row = lax.broadcasted_iota(jnp.int32, (1, lanes), 1)
    target = lax.broadcasted_iota(jnp.int32, (slots, lanes), 1)
    place = lax.broadcasted_iota(jnp.int32, (slots, wide), 1)
    empty = groups_of(slots, row_tiles)
    for half, tiles in ((0, row_tiles), (1, col_tiles)):
        key_col = jnp.where(s_col < count, turned[:slots, half : half + 1], tiles)
        key_row = jnp.where(s_row < count, packed[half : half + 1, :], tiles)
        same = (key_row == key_col) & (s_row < s_col)
        earlier = jnp.sum(same.astype(jnp.int32), axis=1, keepdims=True)
        held = jnp.sum((key_col == target).astype(jnp.int32), axis=0, keepdims=True)
        padded = ((held + (JOIN - 1)) // JOIN) * JOIN
        begin = jnp.sum(jnp.where(target < key_col, padded, 0), axis=1, keepdims=True)
        spot = jnp.where(s_col < count, begin + earlier, -1)
        chosen = (spot == place).astype(jnp.int32)
        source = turned[:slots, 1 - half : 2 - half]
        follows = (earlier > 0).astype(jnp.int32)
        group = spot // JOIN
        end = jnp.max(jnp.where(key_col == target, group, -1), axis=0, keepdims=True)
        base = 4 * half
        tab[base : base + 1, :] = jnp.sum(chosen * (s_col - slots), axis=0, keepdims=True) + slots
        tab[base + 1 : base + 2, :] = jnp.sum(chosen * source, axis=0, keepdims=True)
        tab[base + 2 : base + 3, :] = jnp.sum(chosen * follows, axis=0, keepdims=True)
        tab[base + 3 : base + 4, :lanes] = jnp.where(end >= 0, end, empty)


def layer_kernel(
    n_row,
    n_col,
    live,
    coords,
    row_degree,
    col_degree,
    feat,
    weight,
    cot,
    edges_hbm,
    out,
    grad_feat,
    grad_weight,
    edges,
    turned_edges,
    packed,
    tab_vmem,
    tab,
    row_scale,
    col_scale,
    panel,
    turned_feat,
    upstream,
    sums,
    part,
    back,
    x_buf,
    z_out,
    z_buf,
    c_buf,
    y_out,
    y_buf,
    w_out,
    w1_buf,
    q_out,
    w2_buf,
    q_all,
    w4_buf,
    e_sem,
    t_sem,
    p_send,
    p_recv,
    f_send,
    f_recv,
    u_send,
    u_recv,
    x_send,
    x_recv,
    z_send,
    z_recv,
    c_send,
    c_recv,
    y_send,
    y_recv,
    w_send,
    w1_recv,
    w2_recv,
    w3_recv,
    w4_recv,
):
    row = lax.axis_index("row")
    col = lax.axis_index("col")
    n_y = n_row // CORES
    n_fast = n_col // SLOW
    y, core = row // CORES, lax.rem(row, CORES)
    z, x = col // n_fast, lax.rem(col, n_fast)
    f32, bf16 = jnp.float32, jnp.bfloat16
    other = y * CORES + (1 - core)
    slots, tile = edges_hbm.shape[0], edges_hbm.shape[1]
    tiles_dev = panel.shape[1]
    nodes, width = feat.shape
    block_shape = (tiles_dev, tile, width)

    load_edges = pltpu.make_async_copy(edges_hbm, edges.at[pl.ds(0, slots)], e_sem)
    load_edges.start()
    lanes = row_degree.shape[1]
    parts = nodes // lanes
    packed[...] = jnp.zeros_like(packed)
    packed[0:2, :slots] = coords[...]
    packed[2 : 2 + parts] = row_degree[...]
    packed[2 + parts : 2 + 2 * parts] = col_degree[...]
    table = packed[...]
    turned = jnp.transpose(table)
    for h in range(parts):
        at = slice(h * lanes, (h + 1) * lanes)
        row_scale[at, :] = lax.rsqrt(turned[:, 2 + h : 3 + h].astype(f32))
        first = 2 + parts + h
        col_scale[at, :] = lax.rsqrt(turned[:, first : first + 1].astype(f32))
    own = (row_scale[...] * cot[...].astype(f32)).astype(bf16)
    upstream[pl.ds(col, 1)] = own.reshape((1,) + block_shape)
    greet(n_row, n_col, row, col)

    def up_copy(slot, send, target):
        return remote(upstream.at[slot], upstream.at[slot], u_send.at[send], u_recv.at[slot], (row, target))

    def fan_fast(slot, base):
        for k in range(1, n_fast):
            up_copy(slot, base + k - 1, z * n_fast + lax.rem(x + k, n_fast)).start()

    def fan_fast_wait(slot, base):
        for k in range(1, n_fast):
            up_copy(slot, base + k - 1, z * n_fast + lax.rem(x + k, n_fast)).wait_send()

    up_ok, down_ok = z + 1 < SLOW, z >= 1
    up_base = 2 + n_fast - 1

    @pl.when(up_ok)
    def _():
        up_copy(col, 0, col + n_fast).start()

    @pl.when(down_ok)
    def _():
        up_copy(col, 1, col - n_fast).start()

    fan_fast(col, 2)

    def pass_on(t):
        for side in range(2):
            first = up_base + ((t - 1) * 2 + side) * n_fast
            if side == 0:
                here, slot = z >= t, col - t * n_fast
                onward, target = up_ok, col + n_fast
            else:
                here, slot = z + t < SLOW, col + t * n_fast
                onward, target = down_ok, col - n_fast

            @pl.when(here)
            def _():
                up_copy(slot, first, col).wait_recv()

                @pl.when(onward)
                def _():
                    up_copy(slot, first, target).start()

                fan_fast(slot, first + 1)

    own = jnp.dot(feat[...], weight[...], preferred_element_type=f32)
    panel[pl.ds(row, 1)] = (col_scale[...] * own).astype(bf16).reshape((1,) + block_shape)

    def p_copy(slot, send, target):
        return remote(panel.at[slot], panel.at[slot], p_send.at[send], p_recv.at[slot], (target, col))

    for k in range(1, n_y):
        p_copy(row, k, lax.rem(y + k, n_y) * CORES + core).start()
    p_copy(row, 0, other).start()

    scaled = jnp.transpose(col_scale[...] * feat[...].astype(f32))
    turned_feat[pl.ds(row, 1)] = scaled.astype(bf16)[None]

    def f_copy(slot, send, target):
        return remote(
            turned_feat.at[slot], turned_feat.at[slot], f_send.at[send], f_recv.at[slot], (target, col)
        )

    for k in range(1, n_y):
        f_copy(row, k, lax.rem(y + k, n_y) * CORES + core).start()
    f_copy(row, 0, other).start()
    tab_vmem[...] = jnp.zeros_like(tab_vmem)
    fill_tables(n_col * tiles_dev, n_row * tiles_dev, table, turned, live[0], slots, tab_vmem)
    load_tab = pltpu.make_async_copy(tab_vmem, tab, t_sem)
    load_tab.start()
    sums[sums.shape[0] - 1] = jnp.zeros((tile, width), bf16)
    edges[slots] = jnp.zeros((tile, tile), jnp.int32)
    turned_edges[slots] = jnp.zeros((tile, tile), bf16)
    for k in range(1, n_y):
        slot = lax.rem(y + k, n_y) * CORES + core
        p_copy(slot, n_y - 1 + k, other).wait_recv()
        p_copy(slot, n_y - 1 + k, other).start()
    pass_on(1)
    for k in range(n_y):
        slot = lax.rem(y + k, n_y) * CORES + (1 - core)
        p_copy(slot, 0, other).wait_recv()
    load_edges.wait()
    load_tab.wait()

    def products(base, source, flipped, count):
        def step(n, total):
            keep = tab[base + 2, JOIN * n].astype(f32)
            mats, vals = [], []
            for j in range(JOIN):
                pick, src = tab[base, JOIN * n + j], tab[base + 1, JOIN * n + j]
                mats.append(turned_edges[pick] if flipped else edges[pick].astype(f32).astype(bf16))
                vals.append(source[lax.div(src, tiles_dev), lax.rem(src, tiles_dev)])
            product = jnp.dot(
                jnp.concatenate(mats, axis=1),
                jnp.concatenate(vals, axis=0),
                preferred_element_type=f32,
            )
            total = total * keep + product
            sums[n] = total.astype(bf16)
            return total

        unroll = max(u for u in range(1, 7) if count % u == 0)

        def body(i, total):
            for j in range(unroll):
                total = step(i * unroll + j, total)
            return total

        lax.fori_loop(0, count // unroll, body, jnp.zeros((tile, width), f32))

    turn_unroll = 8 if slots % 16 == 0 else 1

    def turn(lo, hi):
        def body(i, carry):
            for j in range(turn_unroll):
                n = lo + i * turn_unroll + j
                turned_edges[n] = jnp.transpose(edges[n].astype(f32)).astype(bf16)
            return carry

        lax.fori_loop(0, (hi - lo) // turn_unroll, body, 0)

    half = slots // 2
    products(0, panel, False, groups_of(slots, n_col * tiles_dev))
    pass_on(2)
    for k in range(1, n_y):
        slot = lax.rem(y + k, n_y) * CORES + core
        f_copy(slot, n_y - 1 + k, other).wait_recv()
        f_copy(slot, n_y - 1 + k, other).start()
    for block in range(n_col):
        for j in range(tiles_dev):
            part[block, j] = sums[tab[3, block * tiles_dev + j]]

    def x_copy(t, k):
        to = lax.rem(x + k, n_fast)
        block = lax.rem(z + t, SLOW) * n_fast + to
        slot = t * (n_fast - 1) + k - 1
        return remote(
            part.at[block], x_buf.at[slot], x_send.at[slot], x_recv.at[slot], (row, z * n_fast + to)
        )

    order = (2, 3, 1, 0)

    def start_x(i):
        if i >= 2:
            for k in range(1, n_fast):
                x_copy(order[i - 2], k).wait_send()
        for k in range(1, n_fast):
            x_copy(order[i], k).start()

    turn(0, half)
    for t in range(3, SLOW):
        pass_on(t)
    turn(half, slots)

    def z_copy(t):
        return remote(
            z_out.at[t],
            z_buf.at[t],
            z_send.at[t],
            z_recv.at[t],
            (row, lax.rem(z + t, SLOW) * n_fast + x),
        )

    def merge_x(i):
        t = order[i]
        block = lax.rem(z + t, SLOW) * n_fast + x
        total = part[pl.ds(block, 1)][0].astype(f32)
        for k in range(1, n_fast):
            x_copy(t, k).wait_recv()
            total = total + x_buf[t * (n_fast - 1) + k - 1].astype(f32)
        z_out[t] = total.astype(bf16)
        if t:
            z_copy(t).start()

    for k in range(1, n_fast):
        for t in range(SLOW):
            slot = t * n_fast + lax.rem(x + k, n_fast)
            up_copy(slot, 0, col).wait_recv()
    start_x(0)
    products(4, upstream, True, groups_of(slots, n_row * tiles_dev))
    start_x(1)
    for block in range(n_row):
        for j in range(tiles_dev):
            back[block, j] = sums[tab[7, block * tiles_dev + j]]

    def c_copy(k):
        block = lax.rem(y + k, n_y) * CORES + (1 - core)
        return remote(back.at[block], c_buf.at[k], c_send.at[k], c_recv.at[k], (other, col))

    for k in reversed(range(n_y)):
        c_copy(k).start()

    for k in range(n_y):
        slot = lax.rem(y + k, n_y) * CORES + (1 - core)
        f_copy(slot, 0, other).wait_recv()
    quarter = width // n_row
    piece = quarter // n_col
    terms = jnp.zeros((width, width), f32)
    for block in range(n_row):
        terms = terms + jnp.dot(
            turned_feat[block], back[block].reshape((nodes, width)), preferred_element_type=f32
        )
    for r in range(n_row):
        w_out[r] = terms[r * quarter : (r + 1) * quarter]

    def w1_copy(k):
        to = lax.rem(row + k, n_row)
        return remote(w_out.at[to], w1_buf.at[k], w_send.at[k], w1_recv.at[k], (to, col))

    for k in range(1, n_row):
        w1_copy(k).start()

    def y_copy(k):
        return remote(
            y_out.at[k],
            y_buf.at[k],
            y_send.at[k],
            y_recv.at[k],
            (lax.rem(y + k, n_y) * CORES + core, col),
        )

    for k in reversed(range(n_y)):
        c_copy(k).wait_recv()
        block = lax.rem(y + k, n_y) * CORES + core
        total = back[pl.ds(block, 1)][0].astype(f32) + c_buf[k].astype(f32)
        y_out[k] = total.astype(bf16)
        if k:
            y_copy(k).start()

    merge_x(0)
    start_x(2)

    total = w_out[pl.ds(row, 1)][0]
    for k in range(1, n_row):
        w1_copy(k).wait_recv()
        total = total + w1_buf[k]
    for j in range(n_col):
        q_out[j] = total[j * piece : (j + 1) * piece]

    def w2_copy(k):
        to = lax.rem(col + k, n_col)
        return remote(q_out.at[to], w2_buf.at[k], w_send.at[n_row + k], w2_recv.at[k], (row, to))

    for k in range(1, n_col):
        w2_copy(k).start()

    merge_x(1)
    start_x(3)

    total = y_out[0].astype(f32)
    for k in range(1, n_y):
        y_copy(k).wait_recv()
        total = total + y_buf[k].astype(f32)
    grad_panel = (col_scale[...] * total.reshape((nodes, width))).astype(bf16)
    grad_feat[...] = lax.dot_general(
        grad_panel, weight[...], (((1,), (1,)), ((), ())), preferred_element_type=f32
    ).astype(bf16)

    total = q_out[pl.ds(col, 1)][0]
    for k in range(1, n_col):
        w2_copy(k).wait_recv()
        total = total + w2_buf[k]
    q_all[pl.ds(col, 1)] = total[None]

    def w3_copy(k):
        to = lax.rem(col + k, n_col)
        return remote(
            q_all.at[col], q_all.at[col], w_send.at[n_row + n_col + k], w3_recv.at[k], (row, to)
        )

    for k in range(1, n_col):
        w3_copy(k).start()

    merge_x(2)

    for k in range(1, n_col):
        w3_copy(k).wait_recv()
    for j in range(n_col):
        w4_buf[pl.ds(row, 1), j * piece : (j + 1) * piece] = q_all[j][None]

    def w4_copy(k):
        to = lax.rem(row + k, n_row)
        return remote(
            w4_buf.at[row], w4_buf.at[row], w_send.at[n_row + 2 * n_col + k], w4_recv.at[k], (to, col)
        )

    for k in range(1, n_row):
        w4_copy(k).start()

    merge_x(3)

    total = z_out[0].astype(f32)
    for t in order[:3]:
        z_copy(t).wait_recv()
        total = total + z_buf[t].astype(f32)
    out[...] = (row_scale[...] * total.reshape((nodes, width))).astype(bf16)

    f_copy(row, 0, other).wait_send()
    p_copy(row, 0, other).wait_send()
    for k in range(1, n_y):
        f_copy(row, k, other).wait_send()
        f_copy(row, n_y - 1 + k, other).wait_send()
        p_copy(row, k, other).wait_send()
        p_copy(row, n_y - 1 + k, other).wait_send()

    @pl.when(up_ok)
    def _():
        up_copy(col, 0, col).wait_send()

    @pl.when(down_ok)
    def _():
        up_copy(col, 1, col).wait_send()

    fan_fast_wait(col, 2)
    for t in range(1, SLOW):
        for side in range(2):
            first = up_base + ((t - 1) * 2 + side) * n_fast
            if side == 0:
                here, onward = z >= t, up_ok
            else:
                here, onward = z + t < SLOW, down_ok

            @pl.when(here)
            def _():
                @pl.when(onward)
                def _():
                    up_copy(col, first, col).wait_send()

                fan_fast_wait(col, first + 1)

    for k in range(n_y):
        c_copy(k).wait_send()
        if k:
            y_copy(k).wait_send()
    for t in order[2:]:
        for k in range(1, n_fast):
            x_copy(t, k).wait_send()
    for t in order[:3]:
        z_copy(t).wait_send()
    for k in range(1, n_row):
        w1_copy(k).wait_send()
    for k in range(1, n_col):
        w2_copy(k).wait_send()
        w3_copy(k).wait_send()

    for k in range(1, n_row):
        w4_copy(k).wait_recv()
    for r in range(n_row):
        grad_weight[r * quarter : (r + 1) * quarter] = w4_buf[r]
    for k in range(1, n_row):
        w4_copy(k).wait_send()


def hand_over_kernel(a, b, c, a_out, b_out, c_out):
    a_out[...] = a[...]
    b_out[...] = b[...]
    c_out[...] = c[...]


def vmem(n):
    return [pl.BlockSpec(memory_space=pltpu.VMEM)] * n


def shards(
    n_row, n_col, features, weight, tile_coords, tile_live, tile_edges, row_degree, col_degree, cotangent
):
    f32, bf16 = jnp.float32, jnp.bfloat16
    dma, shape = pltpu.SemaphoreType.DMA, jax.ShapeDtypeStruct
    tile = tile_edges.shape[-1]
    slots = tile_edges.shape[2]
    nodes, width = features.shape
    n_y, n_fast = n_row // CORES, n_col // SLOW
    tiles_dev = nodes // tile
    row_tiles = n_col * tiles_dev
    lanes = pl.cdiv(max(slots, row_tiles), 128) * 128
    wide = pl.cdiv(JOIN * groups_of(slots, row_tiles), 128) * 128
    coords = tile_coords[0, 0].T
    degrees = (row_degree.reshape(-1, lanes), col_degree.reshape(-1, lanes))

    quarter = width // n_row
    piece = quarter // n_col
    block = (tiles_dev, tile, width)
    results = pl.pallas_call(
        functools.partial(layer_kernel, n_row, n_col),
        out_shape=(
            shape((nodes, width), bf16),
            shape((nodes, width), bf16),
            shape((width, width), f32),
        ),
        in_specs=[pl.BlockSpec(memory_space=pltpu.SMEM)]
        + vmem(6)
        + [pl.BlockSpec(memory_space=pl.ANY)],
        out_specs=tuple(vmem(3)),
        scratch_shapes=[
            pltpu.VMEM((slots + 1, tile, tile), jnp.int32),
            pltpu.VMEM((slots + 1, tile, tile), bf16),
            pltpu.VMEM((8, lanes), jnp.int32),
            pltpu.VMEM((8, wide), jnp.int32),
            pltpu.SMEM((8, wide), jnp.int32),
            pltpu.VMEM((nodes, 1), f32),
            pltpu.VMEM((nodes, 1), f32),
            pltpu.VMEM((n_row,) + block, bf16),
            pltpu.VMEM((n_row, width, nodes), bf16),
            pltpu.VMEM((n_col,) + block, bf16),
            pltpu.VMEM((groups_of(slots, row_tiles) + 1, tile, width), bf16),
            pltpu.VMEM((n_col,) + block, bf16),
            pltpu.VMEM((n_row,) + block, bf16),
            pltpu.VMEM((SLOW * (n_fast - 1),) + block, bf16),
            pltpu.VMEM((SLOW,) + block, bf16),
            pltpu.VMEM((SLOW,) + block, bf16),
            pltpu.VMEM((n_y,) + block, bf16),
            pltpu.VMEM((n_y,) + block, bf16),
            pltpu.VMEM((n_y,) + block, bf16),
            pltpu.VMEM((n_row, quarter, width), f32),
            pltpu.VMEM((n_row, quarter, width), f32),
            pltpu.VMEM((n_col, piece, width), f32),
            pltpu.VMEM((n_col, piece, width), f32),
            pltpu.VMEM((n_col, piece, width), f32),
            pltpu.VMEM((n_row, quarter, width), f32),
            dma(()),
            dma(()),
            dma((2 * n_y,)),
            dma((n_row,)),
            dma((2 * n_y,)),
            dma((n_row,)),
            dma((2 + n_fast - 1 + 2 * (SLOW - 1) * n_fast,)),
            dma((n_col,)),
            dma((SLOW * (n_fast - 1),)),
            dma((SLOW * (n_fast - 1),)),
            dma((SLOW,)),
            dma((SLOW,)),
            dma((n_y,)),
            dma((n_y,)),
            dma((n_y,)),
            dma((n_y,)),
            dma((2 * n_row + 2 * n_col,)),
            dma((n_row,)),
            dma((n_col,)),
            dma((n_col,)),
            dma((n_row,)),
        ],
        compiler_params=pltpu.CompilerParams(
            collective_id=0, has_side_effects=True, vmem_limit_bytes=56 * MB
        ),
        name="layer",
    )(tile_live.reshape(-1), coords, *degrees, features, weight, cotangent, tile_edges[0, 0])
    return pl.pallas_call(
        hand_over_kernel,
        out_shape=tuple(shape(r.shape, r.dtype) for r in results),
        in_specs=vmem(3),
        out_specs=tuple(vmem(3)),
        compiler_params=pltpu.CompilerParams(vmem_limit_bytes=60 * MB),
        name="hand_over",
    )(*results)


def solution(mesh):
    in_specs = (
        P(("col", "row"), None),
        P(),
        P("row", "col", None, None),
        P("row", "col"),
        P("row", "col", None, None, None),
        P(("row", "col")),
        P(("col", "row")),
        P(("row", "col"), None),
    )
    out_specs = (P(("row", "col"), None), P(("col", "row"), None), P())
    body = functools.partial(shards, mesh.shape["row"], mesh.shape["col"])
    return jax.shard_map(body, mesh=mesh, in_specs=in_specs, out_specs=out_specs, check_vma=False)
```

```python
import functools

import jax
import jax.numpy as jnp
from jax import lax
from jax.experimental import pallas as pl
from jax.experimental.pallas import tpu as pltpu
from jax.sharding import PartitionSpec as P

MESH = pl.DeviceIdType.MESH
CORES = 2
SLOW = 4
JOIN = 4
MB = 1024 * 1024


def greet(n_row, n_col, row, col):
    barrier = pltpu.get_barrier_semaphore()
    for k in range(1, n_row):
        peer = lax.rem(row + k, n_row)
        pl.semaphore_signal(barrier, inc=1, device_id=(peer, col), device_id_type=MESH)
    for k in range(1, n_col):
        peer = lax.rem(col + k, n_col)
        pl.semaphore_signal(barrier, inc=1, device_id=(row, peer), device_id_type=MESH)
    pl.semaphore_wait(barrier, n_row + n_col - 2)


def remote(src, dst, send, recv, target):
    return pltpu.make_async_remote_copy(
        src_ref=src,
        dst_ref=dst,
        send_sem=send,
        recv_sem=recv,
        device_id=target,
        device_id_type=MESH,
    )


def groups_of(slots, tiles):
    return (slots + (JOIN - 1) * tiles) // JOIN


def fill_tables(row_tiles, col_tiles, packed, turned, count, slots, tab):
    lanes, wide = packed.shape[1], tab.shape[1]
    s_col = lax.broadcasted_iota(jnp.int32, (slots, 1), 0)
    s_row = lax.broadcasted_iota(jnp.int32, (1, lanes), 1)
    target = lax.broadcasted_iota(jnp.int32, (slots, lanes), 1)
    place = lax.broadcasted_iota(jnp.int32, (slots, wide), 1)
    empty = groups_of(slots, row_tiles)
    for half, tiles in ((0, row_tiles), (1, col_tiles)):
        key_col = jnp.where(s_col < count, turned[:slots, half : half + 1], tiles)
        key_row = jnp.where(s_row < count, packed[half : half + 1, :], tiles)
        same = (key_row == key_col) & (s_row < s_col)
        earlier = jnp.sum(same.astype(jnp.int32), axis=1, keepdims=True)
        held = jnp.sum((key_col == target).astype(jnp.int32), axis=0, keepdims=True)
        padded = ((held + (JOIN - 1)) // JOIN) * JOIN
        begin = jnp.sum(jnp.where(target < key_col, padded, 0), axis=1, keepdims=True)
        spot = jnp.where(s_col < count, begin + earlier, -1)
        chosen = (spot == place).astype(jnp.int32)
        source = turned[:slots, 1 - half : 2 - half]
        follows = (earlier > 0).astype(jnp.int32)
        group = spot // JOIN
        end = jnp.max(jnp.where(key_col == target, group, -1), axis=0, keepdims=True)
        base = 4 * half
        tab[base : base + 1, :] = jnp.sum(chosen * (s_col - slots), axis=0, keepdims=True) + slots
        tab[base + 1 : base + 2, :] = jnp.sum(chosen * source, axis=0, keepdims=True)
        tab[base + 2 : base + 3, :] = jnp.sum(chosen * follows, axis=0, keepdims=True)
        tab[base + 3 : base + 4, :lanes] = jnp.where(end >= 0, end, empty)


def layer_kernel(
    n_row,
    n_col,
    live,
    coords,
    row_degree,
    col_degree,
    feat,
    weight,
    cot,
    edges_hbm,
    out,
    grad_feat,
    grad_weight,
    edges,
    turned_edges,
    packed,
    tab_vmem,
    tab,
    row_scale,
    col_scale,
    panel,
    turned_feat,
    upstream,
    sums,
    part,
    back,
    f1_buf,
    f2_out,
    f2_buf,
    first_sum,
    x_buf,
    z_out,
    z_buf,
    c_buf,
    y_out,
    y_buf,
    w_out,
    w1_buf,
    q_out,
    w2_buf,
    q_all,
    w4_buf,
    e_sem,
    t_sem,
    p_send,
    p_recv,
    f_send,
    f_recv,
    u_send,
    u_recv,
    f1_send,
    f1_recv,
    f2_send,
    f2_recv,
    x_send,
    x_recv,
    z_send,
    z_recv,
    c_send,
    c_recv,
    y_send,
    y_recv,
    w_send,
    w1_recv,
    w2_recv,
    w3_recv,
    w4_recv,
):
    row = lax.axis_index("row")
    col = lax.axis_index("col")
    n_y = n_row // CORES
    n_fast = n_col // SLOW
    y, core = row // CORES, lax.rem(row, CORES)
    z, x = col // n_fast, lax.rem(col, n_fast)
    f32, bf16 = jnp.float32, jnp.bfloat16
    other = y * CORES + (1 - core)
    slots, tile = edges_hbm.shape[0], edges_hbm.shape[1]
    tiles_dev = panel.shape[1]
    nodes, width = feat.shape
    block_shape = (tiles_dev, tile, width)

    load_edges = pltpu.make_async_copy(edges_hbm, edges.at[pl.ds(0, slots)], e_sem)
    load_edges.start()
    lanes = packed.shape[1]
    parts = nodes // lanes
    packed[...] = jnp.zeros_like(packed)
    packed[0:2, :slots] = coords[...]
    for h in range(parts):
        packed[2 + h, :] = row_degree[pl.ds(h * lanes, lanes)]
        packed[2 + parts + h, :] = col_degree[pl.ds(h * lanes, lanes)]
    table = packed[...]
    turned = jnp.transpose(table)
    for h in range(parts):
        at = slice(h * lanes, (h + 1) * lanes)
        row_scale[at, :] = lax.rsqrt(turned[:, 2 + h : 3 + h].astype(f32))
        first = 2 + parts + h
        col_scale[at, :] = lax.rsqrt(turned[:, first : first + 1].astype(f32))
    own = (row_scale[...] * cot[...].astype(f32)).astype(bf16)
    upstream[pl.ds(col, 1)] = own.reshape((1,) + block_shape)
    greet(n_row, n_col, row, col)

    def up_copy(slot, send, target):
        return remote(upstream.at[slot], upstream.at[slot], u_send.at[send], u_recv.at[slot], (row, target))

    def fan_fast(slot, base):
        for k in range(1, n_fast):
            up_copy(slot, base + k - 1, z * n_fast + lax.rem(x + k, n_fast)).start()

    def fan_fast_wait(slot, base):
        for k in range(1, n_fast):
            up_copy(slot, base + k - 1, z * n_fast + lax.rem(x + k, n_fast)).wait_send()

    up_ok, down_ok = z + 1 < SLOW, z >= 1
    up_base = 2 + n_fast - 1

    @pl.when(up_ok)
    def _():
        up_copy(col, 0, col + n_fast).start()

    @pl.when(down_ok)
    def _():
        up_copy(col, 1, col - n_fast).start()

    fan_fast(col, 2)

    def pass_on(t):
        for side in range(2):
            first = up_base + ((t - 1) * 2 + side) * n_fast
            if side == 0:
                here, slot = z >= t, col - t * n_fast
                onward, target = up_ok, col + n_fast
            else:
                here, slot = z + t < SLOW, col + t * n_fast
                onward, target = down_ok, col - n_fast

            @pl.when(here)
            def _():
                up_copy(slot, first, col).wait_recv()

                @pl.when(onward)
                def _():
                    up_copy(slot, first, target).start()

                fan_fast(slot, first + 1)

    own = jnp.dot(feat[...], weight[...], preferred_element_type=f32)
    panel[pl.ds(row, 1)] = (col_scale[...] * own).astype(bf16).reshape((1,) + block_shape)

    def p_copy(slot, send, target):
        return remote(panel.at[slot], panel.at[slot], p_send.at[send], p_recv.at[slot], (target, col))

    for k in range(1, n_y):
        p_copy(row, k, lax.rem(y + k, n_y) * CORES + core).start()
    p_copy(row, 0, other).start()

    scaled = jnp.transpose(col_scale[...] * feat[...].astype(f32))
    turned_feat[pl.ds(row, 1)] = scaled.astype(bf16)[None]

    def f_copy(slot, send, target):
        return remote(
            turned_feat.at[slot], turned_feat.at[slot], f_send.at[send], f_recv.at[slot], (target, col)
        )

    for k in range(1, n_y):
        f_copy(row, k, lax.rem(y + k, n_y) * CORES + core).start()
    f_copy(row, 0, other).start()
    tab_vmem[...] = jnp.zeros_like(tab_vmem)
    fill_tables(n_col * tiles_dev, n_row * tiles_dev, table, turned, live[0], slots, tab_vmem)
    load_tab = pltpu.make_async_copy(tab_vmem, tab, t_sem)
    load_tab.start()
    sums[sums.shape[0] - 1] = jnp.zeros((tile, width), bf16)
    edges[slots] = jnp.zeros((tile, tile), jnp.int32)
    turned_edges[slots] = jnp.zeros((tile, tile), bf16)
    for k in range(1, n_y):
        slot = lax.rem(y + k, n_y) * CORES + core
        p_copy(slot, n_y - 1 + k, other).wait_recv()
        p_copy(slot, n_y - 1 + k, other).start()
    pass_on(1)
    for k in range(n_y):
        slot = lax.rem(y + k, n_y) * CORES + (1 - core)
        p_copy(slot, 0, other).wait_recv()
    load_edges.wait()
    load_tab.wait()

    def products(base, source, flipped, count):
        def step(n, total):
            keep = tab[base + 2, JOIN * n].astype(f32)
            mats, vals = [], []
            for j in range(JOIN):
                pick, src = tab[base, JOIN * n + j], tab[base + 1, JOIN * n + j]
                mats.append(turned_edges[pick] if flipped else edges[pick].astype(f32).astype(bf16))
                vals.append(source[lax.div(src, tiles_dev), lax.rem(src, tiles_dev)])
            product = jnp.dot(
                jnp.concatenate(mats, axis=1),
                jnp.concatenate(vals, axis=0),
                preferred_element_type=f32,
            )
            total = total * keep + product
            sums[n] = total.astype(bf16)
            return total

        unroll = max(u for u in range(1, 7) if count % u == 0)

        def body(i, total):
            for j in range(unroll):
                total = step(i * unroll + j, total)
            return total

        lax.fori_loop(0, count // unroll, body, jnp.zeros((tile, width), f32))

    turn_unroll = 8 if slots % 16 == 0 else 1

    def turn(lo, hi):
        def body(i, carry):
            for j in range(turn_unroll):
                n = lo + i * turn_unroll + j
                turned_edges[n] = jnp.transpose(edges[n].astype(f32)).astype(bf16)
            return carry

        lax.fori_loop(0, (hi - lo) // turn_unroll, body, 0)

    half = slots // 2
    products(0, panel, False, groups_of(slots, n_col * tiles_dev))
    pass_on(2)
    for k in range(1, n_y):
        slot = lax.rem(y + k, n_y) * CORES + core
        f_copy(slot, n_y - 1 + k, other).wait_recv()
        f_copy(slot, n_y - 1 + k, other).start()
    for block in range(n_col):
        for j in range(tiles_dev):
            part[block, j] = sums[tab[3, block * tiles_dev + j]]

    def x_copy(t, k):
        to = lax.rem(x + k, n_fast)
        block = lax.rem(z + t, SLOW) * n_fast + to
        slot = t * (n_fast - 1) + k - 1
        return remote(
            part.at[block, 1:], x_buf.at[slot], x_send.at[slot], x_recv.at[slot], (row, z * n_fast + to)
        )

    order = (2, 3, 1, 0)

    def start_x(i):
        if i >= 2:
            for k in range(1, n_fast):
                x_copy(order[i - 2], k).wait_send()
        for k in range(1, n_fast):
            x_copy(order[i], k).start()

    turn(0, half)
    for t in range(3, SLOW):
        pass_on(t)

    def f1_copy(t, k):
        slot = t * n_fast + k
        block = lax.rem(z + t, SLOW) * n_fast + lax.rem(x + k, n_fast)
        return remote(
            part.at[block, 0],
            f1_buf.at[slot],
            f1_send.at[slot],
            f1_recv.at[slot],
            (row, lax.rem(z + t, SLOW) * n_fast + x),
        )

    for t in order[:3]:
        for k in range(n_fast):
            f1_copy(t, k).start()
    turn(half, slots)

    def f2_copy(k):
        to = z * n_fast + lax.rem(x + k, n_fast)
        return remote(f2_out.at[k], f2_buf.at[k], f2_send.at[k], f2_recv.at[k], (row, to))

    def merge_f1():
        for k in reversed(range(n_fast)):
            block = z * n_fast + lax.rem(x + k, n_fast)
            total = part[pl.ds(block, 1), 0][0].astype(f32)
            for t in order[:3]:
                f1_copy(t, k).wait_recv()
                total = total + f1_buf[t * n_fast + k].astype(f32)
            if k:
                f2_out[k] = total.astype(bf16)
                f2_copy(k).start()
            else:
                first_sum[...] = total

    def z_copy(t):
        return remote(
            z_out.at[t],
            z_buf.at[t],
            z_send.at[t],
            z_recv.at[t],
            (row, lax.rem(z + t, SLOW) * n_fast + x),
        )

    def merge_x(i):
        t = order[i]
        block = lax.rem(z + t, SLOW) * n_fast + x
        total = part[pl.ds(block, 1), 1:][0].astype(f32)
        for k in range(1, n_fast):
            x_copy(t, k).wait_recv()
            total = total + x_buf[t * (n_fast - 1) + k - 1].astype(f32)
        z_out[t] = total.astype(bf16)
        if t:
            z_copy(t).start()

    for k in range(1, n_fast):
        for t in range(SLOW):
            slot = t * n_fast + lax.rem(x + k, n_fast)
            up_copy(slot, 0, col).wait_recv()
    start_x(0)
    products(4, upstream, True, groups_of(slots, n_row * tiles_dev))
    start_x(1)
    for block in range(n_row):
        for j in range(tiles_dev):
            back[block, j] = sums[tab[7, block * tiles_dev + j]]

    def c_copy(k):
        block = lax.rem(y + k, n_y) * CORES + (1 - core)
        return remote(back.at[block], c_buf.at[k], c_send.at[k], c_recv.at[k], (other, col))

    for k in reversed(range(n_y)):
        c_copy(k).start()

    for k in range(n_y):
        slot = lax.rem(y + k, n_y) * CORES + (1 - core)
        f_copy(slot, 0, other).wait_recv()
    quarter = width // n_row
    piece = quarter // n_col
    terms = jnp.zeros((width, width), f32)
    for block in range(n_row):
        terms = terms + jnp.dot(
            turned_feat[block], back[block].reshape((nodes, width)), preferred_element_type=f32
        )
    for r in range(n_row):
        w_out[r] = terms[r * quarter : (r + 1) * quarter]

    def w1_copy(k):
        to = lax.rem(row + k, n_row)
        return remote(w_out.at[to], w1_buf.at[k], w_send.at[k], w1_recv.at[k], (to, col))

    for k in range(1, n_row):
        w1_copy(k).start()

    def y_copy(k):
        return remote(
            y_out.at[k],
            y_buf.at[k],
            y_send.at[k],
            y_recv.at[k],
            (lax.rem(y + k, n_y) * CORES + core, col),
        )

    for k in reversed(range(n_y)):
        c_copy(k).wait_recv()
        block = lax.rem(y + k, n_y) * CORES + core
        total = back[pl.ds(block, 1)][0].astype(f32) + c_buf[k].astype(f32)
        y_out[k] = total.astype(bf16)
        if k:
            y_copy(k).start()

    merge_x(0)
    start_x(2)

    total = w_out[pl.ds(row, 1)][0]
    for k in range(1, n_row):
        w1_copy(k).wait_recv()
        total = total + w1_buf[k]
    for j in range(n_col):
        q_out[j] = total[j * piece : (j + 1) * piece]

    def w2_copy(k):
        to = lax.rem(col + k, n_col)
        return remote(q_out.at[to], w2_buf.at[k], w_send.at[n_row + k], w2_recv.at[k], (row, to))

    for k in range(1, n_col):
        w2_copy(k).start()

    merge_x(1)
    start_x(3)
    merge_f1()
    merge_x(2)

    total = y_out[0].astype(f32)
    for k in range(1, n_y):
        y_copy(k).wait_recv()
        total = total + y_buf[k].astype(f32)
    grad_panel = (col_scale[...] * total.reshape((nodes, width))).astype(bf16)
    grad_feat[...] = lax.dot_general(
        grad_panel, weight[...], (((1,), (1,)), ((), ())), preferred_element_type=f32
    ).astype(bf16)

    total = q_out[pl.ds(col, 1)][0]
    for k in range(1, n_col):
        w2_copy(k).wait_recv()
        total = total + w2_buf[k]
    q_all[pl.ds(col, 1)] = total[None]

    def w3_copy(k):
        to = lax.rem(col + k, n_col)
        return remote(
            q_all.at[col], q_all.at[col], w_send.at[n_row + n_col + k], w3_recv.at[k], (row, to)
        )

    for k in range(1, n_col):
        w3_copy(k).start()

    merge_x(3)

    for k in range(1, n_col):
        w3_copy(k).wait_recv()
    for j in range(n_col):
        w4_buf[pl.ds(row, 1), j * piece : (j + 1) * piece] = q_all[j][None]

    def w4_copy(k):
        to = lax.rem(row + k, n_row)
        return remote(
            w4_buf.at[row], w4_buf.at[row], w_send.at[n_row + 2 * n_col + k], w4_recv.at[k], (to, col)
        )

    for k in range(1, n_row):
        w4_copy(k).start()

    total = z_out[0].astype(f32)
    for t in order[:3]:
        z_copy(t).wait_recv()
        total = total + z_buf[t].astype(f32)
    rest_scale = row_scale[tile:, :]
    out[tile:, :] = (rest_scale * total.reshape((nodes - tile, width))).astype(bf16)
    total = first_sum[...]
    for k in range(1, n_fast):
        f2_copy(k).wait_recv()
        total = total + f2_buf[k].astype(f32)
    out[:tile, :] = (row_scale[:tile, :] * total).astype(bf16)

    f_copy(row, 0, other).wait_send()
    p_copy(row, 0, other).wait_send()
    for k in range(1, n_y):
        f_copy(row, k, other).wait_send()
        f_copy(row, n_y - 1 + k, other).wait_send()
        p_copy(row, k, other).wait_send()
        p_copy(row, n_y - 1 + k, other).wait_send()

    @pl.when(up_ok)
    def _():
        up_copy(col, 0, col).wait_send()

    @pl.when(down_ok)
    def _():
        up_copy(col, 1, col).wait_send()

    fan_fast_wait(col, 2)
    for t in range(1, SLOW):
        for side in range(2):
            first = up_base + ((t - 1) * 2 + side) * n_fast
            if side == 0:
                here, onward = z >= t, up_ok
            else:
                here, onward = z + t < SLOW, down_ok

            @pl.when(here)
            def _():
                @pl.when(onward)
                def _():
                    up_copy(col, first, col).wait_send()

                fan_fast_wait(col, first + 1)

    for k in range(n_y):
        c_copy(k).wait_send()
        if k:
            y_copy(k).wait_send()
    for t in order[2:]:
        for k in range(1, n_fast):
            x_copy(t, k).wait_send()
    for t in order[:3]:
        z_copy(t).wait_send()
        for k in range(n_fast):
            f1_copy(t, k).wait_send()
    for k in range(1, n_fast):
        f2_copy(k).wait_send()
    for k in range(1, n_row):
        w1_copy(k).wait_send()
    for k in range(1, n_col):
        w2_copy(k).wait_send()
        w3_copy(k).wait_send()

    for k in range(1, n_row):
        w4_copy(k).wait_recv()
    for r in range(n_row):
        grad_weight[r * quarter : (r + 1) * quarter] = w4_buf[r]
    for k in range(1, n_row):
        w4_copy(k).wait_send()


def hand_over_kernel(a, b, c, a_out, b_out, c_out):
    a_out[...] = a[...]
    b_out[...] = b[...]
    c_out[...] = c[...]


def vmem(n):
    return [pl.BlockSpec(memory_space=pltpu.VMEM)] * n


def shards(
    n_row, n_col, features, weight, tile_coords, tile_live, tile_edges, row_degree, col_degree, cotangent
):
    f32, bf16 = jnp.float32, jnp.bfloat16
    dma, shape = pltpu.SemaphoreType.DMA, jax.ShapeDtypeStruct
    tile = tile_edges.shape[-1]
    slots = tile_edges.shape[2]
    nodes, width = features.shape
    n_y, n_fast = n_row // CORES, n_col // SLOW
    tiles_dev = nodes // tile
    row_tiles = n_col * tiles_dev
    lanes = pl.cdiv(max(slots, row_tiles), 128) * 128
    wide = pl.cdiv(JOIN * groups_of(slots, row_tiles), 128) * 128
    coords = tile_coords[0, 0].T

    quarter = width // n_row
    piece = quarter // n_col
    block = (tiles_dev, tile, width)
    rest = (tiles_dev - 1, tile, width)
    results = pl.pallas_call(
        functools.partial(layer_kernel, n_row, n_col),
        out_shape=(
            shape((nodes, width), bf16),
            shape((nodes, width), bf16),
            shape((width, width), f32),
        ),
        in_specs=[pl.BlockSpec(memory_space=pltpu.SMEM)]
        + vmem(6)
        + [pl.BlockSpec(memory_space=pl.ANY)],
        out_specs=tuple(vmem(3)),
        scratch_shapes=[
            pltpu.VMEM((slots + 1, tile, tile), jnp.int32),
            pltpu.VMEM((slots + 1, tile, tile), bf16),
            pltpu.VMEM((8, lanes), jnp.int32),
            pltpu.VMEM((8, wide), jnp.int32),
            pltpu.SMEM((8, wide), jnp.int32),
            pltpu.VMEM((nodes, 1), f32),
            pltpu.VMEM((nodes, 1), f32),
            pltpu.VMEM((n_row,) + block, bf16),
            pltpu.VMEM((n_row, width, nodes), bf16),
            pltpu.VMEM((n_col,) + block, bf16),
            pltpu.VMEM((groups_of(slots, row_tiles) + 1, tile, width), bf16),
            pltpu.VMEM((n_col,) + block, bf16),
            pltpu.VMEM((n_row,) + block, bf16),
            pltpu.VMEM((SLOW * n_fast, tile, width), bf16),
            pltpu.VMEM((n_fast, tile, width), bf16),
            pltpu.VMEM((n_fast, tile, width), bf16),
            pltpu.VMEM((tile, width), f32),
            pltpu.VMEM((SLOW * (n_fast - 1),) + rest, bf16),
            pltpu.VMEM((SLOW,) + rest, bf16),
            pltpu.VMEM((SLOW,) + rest, bf16),
            pltpu.VMEM((n_y,) + block, bf16),
            pltpu.VMEM((n_y,) + block, bf16),
            pltpu.VMEM((n_y,) + block, bf16),
            pltpu.VMEM((n_row, quarter, width), f32),
            pltpu.VMEM((n_row, quarter, width), f32),
            pltpu.VMEM((n_col, piece, width), f32),
            pltpu.VMEM((n_col, piece, width), f32),
            pltpu.VMEM((n_col, piece, width), f32),
            pltpu.VMEM((n_row, quarter, width), f32),
            dma(()),
            dma(()),
            dma((2 * n_y,)),
            dma((n_row,)),
            dma((2 * n_y,)),
            dma((n_row,)),
            dma((2 + n_fast - 1 + 2 * (SLOW - 1) * n_fast,)),
            dma((n_col,)),
            dma((SLOW * n_fast,)),
            dma((SLOW * n_fast,)),
            dma((n_fast,)),
            dma((n_fast,)),
            dma((SLOW * (n_fast - 1),)),
            dma((SLOW * (n_fast - 1),)),
            dma((SLOW,)),
            dma((SLOW,)),
            dma((n_y,)),
            dma((n_y,)),
            dma((n_y,)),
            dma((n_y,)),
            dma((2 * n_row + 2 * n_col,)),
            dma((n_row,)),
            dma((n_col,)),
            dma((n_col,)),
            dma((n_row,)),
        ],
        compiler_params=pltpu.CompilerParams(
            collective_id=0, has_side_effects=True, vmem_limit_bytes=56 * MB
        ),
        name="layer",
    )(tile_live.reshape(-1), coords, row_degree, col_degree, features, weight, cotangent, tile_edges[0, 0])
    return pl.pallas_call(
        hand_over_kernel,
        out_shape=tuple(shape(r.shape, r.dtype) for r in results),
        in_specs=vmem(3),
        out_specs=tuple(vmem(3)),
        compiler_params=pltpu.CompilerParams(vmem_limit_bytes=60 * MB),
        name="hand_over",
    )(*results)


def solution(mesh):
    in_specs = (
        P(("col", "row"), None),
        P(),
        P("row", "col", None, None),
        P("row", "col"),
        P("row", "col", None, None, None),
        P(("row", "col")),
        P(("col", "row")),
        P(("row", "col"), None),
    )
    out_specs = (P(("row", "col"), None), P(("col", "row"), None), P())
    body = functools.partial(shards, mesh.shape["row"], mesh.shape["col"])
    return jax.shard_map(body, mesh=mesh, in_specs=in_specs, out_specs=out_specs, check_vma=False)
```

```python
import functools

import jax
import jax.numpy as jnp
from jax import lax
from jax.experimental import pallas as pl
from jax.experimental.pallas import tpu as pltpu
from jax.sharding import PartitionSpec as P

MESH = pl.DeviceIdType.MESH
CORES = 2
SLOW = 4
JOIN = 4
MB = 1024 * 1024


def greet(n_row, n_col, row, col):
    barrier = pltpu.get_barrier_semaphore()
    for k in range(1, n_row):
        peer = lax.rem(row + k, n_row)
        pl.semaphore_signal(barrier, inc=1, device_id=(peer, col), device_id_type=MESH)
    for k in range(1, n_col):
        peer = lax.rem(col + k, n_col)
        pl.semaphore_signal(barrier, inc=1, device_id=(row, peer), device_id_type=MESH)
    pl.semaphore_wait(barrier, n_row + n_col - 2)


def remote(src, dst, send, recv, target):
    return pltpu.make_async_remote_copy(
        src_ref=src,
        dst_ref=dst,
        send_sem=send,
        recv_sem=recv,
        device_id=target,
        device_id_type=MESH,
    )


def groups_of(slots, tiles):
    return (slots + (JOIN - 1) * tiles) // JOIN


def fill_tables(row_tiles, col_tiles, packed, turned, count, slots, tab):
    lanes, wide = packed.shape[1], tab.shape[1]
    s_col = lax.broadcasted_iota(jnp.int32, (slots, 1), 0)
    s_row = lax.broadcasted_iota(jnp.int32, (1, lanes), 1)
    target = lax.broadcasted_iota(jnp.int32, (slots, lanes), 1)
    place = lax.broadcasted_iota(jnp.int32, (slots, wide), 1)
    empty = groups_of(slots, row_tiles)
    for half, tiles in ((0, row_tiles), (1, col_tiles)):
        key_col = jnp.where(s_col < count, turned[:slots, half : half + 1], tiles)
        key_row = jnp.where(s_row < count, packed[half : half + 1, :], tiles)
        same = (key_row == key_col) & (s_row < s_col)
        earlier = jnp.sum(same.astype(jnp.int32), axis=1, keepdims=True)
        held = jnp.sum((key_col == target).astype(jnp.int32), axis=0, keepdims=True)
        padded = ((held + (JOIN - 1)) // JOIN) * JOIN
        begin = jnp.sum(jnp.where(target < key_col, padded, 0), axis=1, keepdims=True)
        spot = jnp.where(s_col < count, begin + earlier, -1)
        chosen = (spot == place).astype(jnp.int32)
        source = turned[:slots, 1 - half : 2 - half]
        follows = (earlier > 0).astype(jnp.int32)
        group = spot // JOIN
        end = jnp.max(jnp.where(key_col == target, group, -1), axis=0, keepdims=True)
        base = 4 * half
        tab[base : base + 1, :] = jnp.sum(chosen * (s_col - slots), axis=0, keepdims=True) + slots
        tab[base + 1 : base + 2, :] = jnp.sum(chosen * source, axis=0, keepdims=True)
        tab[base + 2 : base + 3, :] = jnp.sum(chosen * follows, axis=0, keepdims=True)
        tab[base + 3 : base + 4, :lanes] = jnp.where(end >= 0, end, empty)


def layer_kernel(
    n_row,
    n_col,
    live,
    coords,
    row_degree,
    col_degree,
    feat,
    weight,
    cot,
    edges_hbm,
    out,
    grad_feat,
    grad_weight,
    edges,
    turned_edges,
    packed,
    tab_vmem,
    tab,
    row_scale,
    col_scale,
    panel,
    turned_feat,
    upstream,
    sums,
    part,
    back,
    f1_buf,
    f2_out,
    f2_buf,
    first_sum,
    x_buf,
    z_out,
    z_buf,
    c_buf,
    y_out,
    y_buf,
    w_out,
    w1_buf,
    q_out,
    w2_buf,
    q_all,
    w_stage,
    w4_buf,
    e_sem,
    t_sem,
    p_send,
    p_recv,
    f_send,
    f_recv,
    u_send,
    u_recv,
    f1_send,
    f1_recv,
    f2_send,
    f2_recv,
    x_send,
    x_recv,
    z_send,
    z_recv,
    c_send,
    c_recv,
    y_send,
    y_recv,
    w_send,
    w1_recv,
    w2_recv,
    w3_recv,
    w4_recv,
):
    row = lax.axis_index("row")
    col = lax.axis_index("col")
    n_y = n_row // CORES
    n_fast = n_col // SLOW
    y, core = row // CORES, lax.rem(row, CORES)
    z, x = col // n_fast, lax.rem(col, n_fast)
    f32, bf16 = jnp.float32, jnp.bfloat16
    other = y * CORES + (1 - core)
    slots, tile = edges_hbm.shape[0], edges_hbm.shape[1]
    tiles_dev = panel.shape[1]
    nodes, width = feat.shape
    block_shape = (tiles_dev, tile, width)

    load_edges = pltpu.make_async_copy(edges_hbm, edges.at[pl.ds(0, slots)], e_sem)
    load_edges.start()
    lanes = packed.shape[1]
    parts = nodes // lanes
    packed[...] = jnp.zeros_like(packed)
    packed[0:2, :slots] = coords[...]
    for h in range(parts):
        packed[2 + h, :] = row_degree[pl.ds(h * lanes, lanes)]
        packed[2 + parts + h, :] = col_degree[pl.ds(h * lanes, lanes)]
    table = packed[...]
    turned = jnp.transpose(table)
    for h in range(parts):
        at = slice(h * lanes, (h + 1) * lanes)
        row_scale[at, :] = lax.rsqrt(turned[:, 2 + h : 3 + h].astype(f32))
        first = 2 + parts + h
        col_scale[at, :] = lax.rsqrt(turned[:, first : first + 1].astype(f32))
    own = (row_scale[...] * cot[...].astype(f32)).astype(bf16)
    upstream[pl.ds(col, 1)] = own.reshape((1,) + block_shape)
    greet(n_row, n_col, row, col)

    def up_copy(slot, send, target):
        return remote(upstream.at[slot], upstream.at[slot], u_send.at[send], u_recv.at[slot], (row, target))

    def fan_fast(slot, base):
        for k in range(1, n_fast):
            up_copy(slot, base + k - 1, z * n_fast + lax.rem(x + k, n_fast)).start()

    def fan_fast_wait(slot, base):
        for k in range(1, n_fast):
            up_copy(slot, base + k - 1, z * n_fast + lax.rem(x + k, n_fast)).wait_send()

    up_ok, down_ok = z + 1 < SLOW, z >= 1
    up_base = 2 + n_fast - 1

    @pl.when(up_ok)
    def _():
        up_copy(col, 0, col + n_fast).start()

    @pl.when(down_ok)
    def _():
        up_copy(col, 1, col - n_fast).start()

    fan_fast(col, 2)

    def pass_on(t):
        for side in range(2):
            first = up_base + ((t - 1) * 2 + side) * n_fast
            if side == 0:
                here, slot = z >= t, col - t * n_fast
                onward, target = up_ok, col + n_fast
            else:
                here, slot = z + t < SLOW, col + t * n_fast
                onward, target = down_ok, col - n_fast

            @pl.when(here)
            def _():
                up_copy(slot, first, col).wait_recv()

                @pl.when(onward)
                def _():
                    up_copy(slot, first, target).start()

                fan_fast(slot, first + 1)

    own = jnp.dot(feat[...], weight[...], preferred_element_type=f32)
    panel[pl.ds(row, 1)] = (col_scale[...] * own).astype(bf16).reshape((1,) + block_shape)

    def p_copy(slot, send, target):
        return remote(panel.at[slot], panel.at[slot], p_send.at[send], p_recv.at[slot], (target, col))

    for k in range(1, n_y):
        p_copy(row, k, lax.rem(y + k, n_y) * CORES + core).start()
    p_copy(row, 0, other).start()

    scaled = jnp.transpose(col_scale[...] * feat[...].astype(f32))
    turned_feat[pl.ds(row, 1)] = scaled.astype(bf16)[None]

    def f_copy(slot, send, target):
        return remote(
            turned_feat.at[slot], turned_feat.at[slot], f_send.at[send], f_recv.at[slot], (target, col)
        )

    for k in range(1, n_y):
        f_copy(row, k, lax.rem(y + k, n_y) * CORES + core).start()
    f_copy(row, 0, other).start()
    tab_vmem[...] = jnp.zeros_like(tab_vmem)
    fill_tables(n_col * tiles_dev, n_row * tiles_dev, table, turned, live[0], slots, tab_vmem)
    load_tab = pltpu.make_async_copy(tab_vmem, tab, t_sem)
    load_tab.start()
    sums[sums.shape[0] - 1] = jnp.zeros((tile, width), bf16)
    edges[slots] = jnp.zeros((tile, tile), jnp.int32)
    turned_edges[slots] = jnp.zeros((tile, tile), bf16)
    for k in range(1, n_y):
        slot = lax.rem(y + k, n_y) * CORES + core
        p_copy(slot, n_y - 1 + k, other).wait_recv()
        p_copy(slot, n_y - 1 + k, other).start()
    pass_on(1)
    for k in range(n_y):
        slot = lax.rem(y + k, n_y) * CORES + (1 - core)
        p_copy(slot, 0, other).wait_recv()
    load_edges.wait()
    load_tab.wait()

    def products(base, source, flipped, count):
        def step(n, total):
            keep = tab[base + 2, JOIN * n].astype(f32)
            mats, vals = [], []
            for j in range(JOIN):
                pick, src = tab[base, JOIN * n + j], tab[base + 1, JOIN * n + j]
                mats.append(turned_edges[pick] if flipped else edges[pick].astype(f32).astype(bf16))
                vals.append(source[lax.div(src, tiles_dev), lax.rem(src, tiles_dev)])
            product = jnp.dot(
                jnp.concatenate(mats, axis=1),
                jnp.concatenate(vals, axis=0),
                preferred_element_type=f32,
            )
            total = total * keep + product
            sums[n] = total.astype(bf16)
            return total

        unroll = max(u for u in range(1, 7) if count % u == 0)

        def body(i, total):
            for j in range(unroll):
                total = step(i * unroll + j, total)
            return total

        lax.fori_loop(0, count // unroll, body, jnp.zeros((tile, width), f32))

    turn_unroll = 8 if slots % 16 == 0 else 1

    def turn(lo, hi):
        def body(i, carry):
            for j in range(turn_unroll):
                n = lo + i * turn_unroll + j
                turned_edges[n] = jnp.transpose(edges[n].astype(f32)).astype(bf16)
            return carry

        lax.fori_loop(0, (hi - lo) // turn_unroll, body, 0)

    half = slots // 2
    products(0, panel, False, groups_of(slots, n_col * tiles_dev))
    pass_on(2)
    for k in range(1, n_y):
        slot = lax.rem(y + k, n_y) * CORES + core
        f_copy(slot, n_y - 1 + k, other).wait_recv()
        f_copy(slot, n_y - 1 + k, other).start()
    for block in range(n_col):
        for j in range(tiles_dev):
            part[block, j] = sums[tab[3, block * tiles_dev + j]]

    def x_copy(t, k):
        to = lax.rem(x + k, n_fast)
        block = lax.rem(z + t, SLOW) * n_fast + to
        slot = t * (n_fast - 1) + k - 1
        return remote(
            part.at[block, 1:], x_buf.at[slot], x_send.at[slot], x_recv.at[slot], (row, z * n_fast + to)
        )

    order = (2, 3, 1, 0)

    def start_x(i):
        if i >= 2:
            for k in range(1, n_fast):
                x_copy(order[i - 2], k).wait_send()
        for k in range(1, n_fast):
            x_copy(order[i], k).start()

    turn(0, half)
    for t in range(3, SLOW):
        pass_on(t)

    def f1_copy(t, k):
        slot = t * n_fast + k
        block = lax.rem(z + t, SLOW) * n_fast + lax.rem(x + k, n_fast)
        return remote(
            part.at[block, 0],
            f1_buf.at[slot],
            f1_send.at[slot],
            f1_recv.at[slot],
            (row, lax.rem(z + t, SLOW) * n_fast + x),
        )

    for t in order[:3]:
        for k in range(n_fast):
            f1_copy(t, k).start()
    turn(half, slots)

    def f2_copy(k):
        to = z * n_fast + lax.rem(x + k, n_fast)
        return remote(f2_out.at[k], f2_buf.at[k], f2_send.at[k], f2_recv.at[k], (row, to))

    def merge_f1():
        for k in reversed(range(n_fast)):
            block = z * n_fast + lax.rem(x + k, n_fast)
            total = part[pl.ds(block, 1), 0][0].astype(f32)
            for t in order[:3]:
                f1_copy(t, k).wait_recv()
                total = total + f1_buf[t * n_fast + k].astype(f32)
            if k:
                f2_out[k] = total.astype(bf16)
                f2_copy(k).start()
            else:
                first_sum[...] = total

    def z_copy(t):
        return remote(
            z_out.at[t],
            z_buf.at[t],
            z_send.at[t],
            z_recv.at[t],
            (row, lax.rem(z + t, SLOW) * n_fast + x),
        )

    def merge_x(i):
        t = order[i]
        block = lax.rem(z + t, SLOW) * n_fast + x
        total = part[pl.ds(block, 1), 1:][0].astype(f32)
        for k in range(1, n_fast):
            x_copy(t, k).wait_recv()
            total = total + x_buf[t * (n_fast - 1) + k - 1].astype(f32)
        z_out[t] = total.astype(bf16)
        if t:
            z_copy(t).start()

    for k in range(1, n_fast):
        for t in range(SLOW):
            slot = t * n_fast + lax.rem(x + k, n_fast)
            up_copy(slot, 0, col).wait_recv()
    start_x(0)
    products(4, upstream, True, groups_of(slots, n_row * tiles_dev))
    start_x(1)
    for block in range(n_row):
        for j in range(tiles_dev):
            back[block, j] = sums[tab[7, block * tiles_dev + j]]

    def c_copy(k):
        block = lax.rem(y + k, n_y) * CORES + (1 - core)
        return remote(back.at[block], c_buf.at[k], c_send.at[k], c_recv.at[k], (other, col))

    for k in reversed(range(n_y)):
        c_copy(k).start()

    for k in range(n_y):
        slot = lax.rem(y + k, n_y) * CORES + (1 - core)
        f_copy(slot, 0, other).wait_recv()
    quarter = width // n_row
    piece = quarter // n_col
    terms = jnp.zeros((width, width), f32)
    for block in range(n_row):
        terms = terms + jnp.dot(
            turned_feat[block], back[block].reshape((nodes, width)), preferred_element_type=f32
        )
    for r in range(n_row):
        w_out[r] = terms[r * quarter : (r + 1) * quarter].astype(bf16)

    def w1_copy(k):
        to = lax.rem(row + k, n_row)
        return remote(w_out.at[to], w1_buf.at[k], w_send.at[k], w1_recv.at[k], (to, col))

    for k in range(1, n_row):
        w1_copy(k).start()

    def y_copy(k):
        return remote(
            y_out.at[k],
            y_buf.at[k],
            y_send.at[k],
            y_recv.at[k],
            (lax.rem(y + k, n_y) * CORES + core, col),
        )

    for k in reversed(range(n_y)):
        c_copy(k).wait_recv()
        block = lax.rem(y + k, n_y) * CORES + core
        total = back[pl.ds(block, 1)][0].astype(f32) + c_buf[k].astype(f32)
        y_out[k] = total.astype(bf16)
        if k:
            y_copy(k).start()

    merge_x(0)
    start_x(2)

    total = w_out[pl.ds(row, 1)][0].astype(f32)
    for k in range(1, n_row):
        w1_copy(k).wait_recv()
        total = total + w1_buf[k].astype(f32)
    for j in range(n_col):
        q_out[j] = total[j * piece : (j + 1) * piece]

    def w2_copy(k):
        to = lax.rem(col + k, n_col)
        return remote(q_out.at[to], w2_buf.at[k], w_send.at[n_row + k], w2_recv.at[k], (row, to))

    for k in range(1, n_col):
        w2_copy(k).start()

    merge_x(1)
    start_x(3)
    merge_f1()
    merge_x(2)

    total = y_out[0].astype(f32)
    for k in range(1, n_y):
        y_copy(k).wait_recv()
        total = total + y_buf[k].astype(f32)
    grad_panel = (col_scale[...] * total.reshape((nodes, width))).astype(bf16)
    grad_feat[...] = lax.dot_general(
        grad_panel, weight[...], (((1,), (1,)), ((), ())), preferred_element_type=f32
    ).astype(bf16)

    total = q_out[pl.ds(col, 1)][0]
    for k in range(1, n_col):
        w2_copy(k).wait_recv()
        total = total + w2_buf[k]
    q_all[pl.ds(col, 1)] = total[None]

    def w3_copy(k):
        to = lax.rem(col + k, n_col)
        return remote(
            q_all.at[col], q_all.at[col], w_send.at[n_row + n_col + k], w3_recv.at[k], (row, to)
        )

    for k in range(1, n_col):
        w3_copy(k).start()

    merge_x(3)

    for k in range(1, n_col):
        w3_copy(k).wait_recv()
    for j in range(n_col):
        w_stage[j * piece : (j + 1) * piece] = q_all[j]
    w4_buf[pl.ds(row, 1)] = w_stage[...].astype(bf16)[None]

    def w4_copy(k):
        to = lax.rem(row + k, n_row)
        return remote(
            w4_buf.at[row], w4_buf.at[row], w_send.at[n_row + 2 * n_col + k], w4_recv.at[k], (to, col)
        )

    for k in range(1, n_row):
        w4_copy(k).start()

    total = z_out[0].astype(f32)
    for t in order[:3]:
        z_copy(t).wait_recv()
        total = total + z_buf[t].astype(f32)
    rest_scale = row_scale[tile:, :]
    out[tile:, :] = (rest_scale * total.reshape((nodes - tile, width))).astype(bf16)
    total = first_sum[...]
    for k in range(1, n_fast):
        f2_copy(k).wait_recv()
        total = total + f2_buf[k].astype(f32)
    out[:tile, :] = (row_scale[:tile, :] * total).astype(bf16)

    f_copy(row, 0, other).wait_send()
    p_copy(row, 0, other).wait_send()
    for k in range(1, n_y):
        f_copy(row, k, other).wait_send()
        f_copy(row, n_y - 1 + k, other).wait_send()
        p_copy(row, k, other).wait_send()
        p_copy(row, n_y - 1 + k, other).wait_send()

    @pl.when(up_ok)
    def _():
        up_copy(col, 0, col).wait_send()

    @pl.when(down_ok)
    def _():
        up_copy(col, 1, col).wait_send()

    fan_fast_wait(col, 2)
    for t in range(1, SLOW):
        for side in range(2):
            first = up_base + ((t - 1) * 2 + side) * n_fast
            if side == 0:
                here, onward = z >= t, up_ok
            else:
                here, onward = z + t < SLOW, down_ok

            @pl.when(here)
            def _():
                @pl.when(onward)
                def _():
                    up_copy(col, first, col).wait_send()

                fan_fast_wait(col, first + 1)

    for k in range(n_y):
        c_copy(k).wait_send()
        if k:
            y_copy(k).wait_send()
    for t in order[2:]:
        for k in range(1, n_fast):
            x_copy(t, k).wait_send()
    for t in order[:3]:
        z_copy(t).wait_send()
        for k in range(n_fast):
            f1_copy(t, k).wait_send()
    for k in range(1, n_fast):
        f2_copy(k).wait_send()
    for k in range(1, n_row):
        w1_copy(k).wait_send()
    for k in range(1, n_col):
        w2_copy(k).wait_send()
        w3_copy(k).wait_send()

    for k in range(1, n_row):
        w4_copy(k).wait_recv()
    for r in range(n_row):
        grad_weight[r * quarter : (r + 1) * quarter] = w4_buf[r].astype(f32)
    for k in range(1, n_row):
        w4_copy(k).wait_send()


def hand_over_kernel(a, b, c, a_out, b_out, c_out):
    a_out[...] = a[...]
    b_out[...] = b[...]
    c_out[...] = c[...]


def vmem(n):
    return [pl.BlockSpec(memory_space=pltpu.VMEM)] * n


def shards(
    n_row, n_col, features, weight, tile_coords, tile_live, tile_edges, row_degree, col_degree, cotangent
):
    f32, bf16 = jnp.float32, jnp.bfloat16
    dma, shape = pltpu.SemaphoreType.DMA, jax.ShapeDtypeStruct
    tile = tile_edges.shape[-1]
    slots = tile_edges.shape[2]
    nodes, width = features.shape
    n_y, n_fast = n_row // CORES, n_col // SLOW
    tiles_dev = nodes // tile
    row_tiles = n_col * tiles_dev
    lanes = pl.cdiv(max(slots, row_tiles), 128) * 128
    wide = pl.cdiv(JOIN * groups_of(slots, row_tiles), 128) * 128
    coords = tile_coords[0, 0].T

    quarter = width // n_row
    piece = quarter // n_col
    block = (tiles_dev, tile, width)
    rest = (tiles_dev - 1, tile, width)
    results = pl.pallas_call(
        functools.partial(layer_kernel, n_row, n_col),
        out_shape=(
            shape((nodes, width), bf16),
            shape((nodes, width), bf16),
            shape((width, width), f32),
        ),
        in_specs=[pl.BlockSpec(memory_space=pltpu.SMEM)]
        + vmem(6)
        + [pl.BlockSpec(memory_space=pl.ANY)],
        out_specs=tuple(vmem(3)),
        scratch_shapes=[
            pltpu.VMEM((slots + 1, tile, tile), jnp.int32),
            pltpu.VMEM((slots + 1, tile, tile), bf16),
            pltpu.VMEM((8, lanes), jnp.int32),
            pltpu.VMEM((8, wide), jnp.int32),
            pltpu.SMEM((8, wide), jnp.int32),
            pltpu.VMEM((nodes, 1), f32),
            pltpu.VMEM((nodes, 1), f32),
            pltpu.VMEM((n_row,) + block, bf16),
            pltpu.VMEM((n_row, width, nodes), bf16),
            pltpu.VMEM((n_col,) + block, bf16),
            pltpu.VMEM((groups_of(slots, row_tiles) + 1, tile, width), bf16),
            pltpu.VMEM((n_col,) + block, bf16),
            pltpu.VMEM((n_row,) + block, bf16),
            pltpu.VMEM((SLOW * n_fast, tile, width), bf16),
            pltpu.VMEM((n_fast, tile, width), bf16),
            pltpu.VMEM((n_fast, tile, width), bf16),
            pltpu.VMEM((tile, width), f32),
            pltpu.VMEM((SLOW * (n_fast - 1),) + rest, bf16),
            pltpu.VMEM((SLOW,) + rest, bf16),
            pltpu.VMEM((SLOW,) + rest, bf16),
            pltpu.VMEM((n_y,) + block, bf16),
            pltpu.VMEM((n_y,) + block, bf16),
            pltpu.VMEM((n_y,) + block, bf16),
            pltpu.VMEM((n_row, quarter, width), bf16),
            pltpu.VMEM((n_row, quarter, width), bf16),
            pltpu.VMEM((n_col, piece, width), f32),
            pltpu.VMEM((n_col, piece, width), f32),
            pltpu.VMEM((n_col, piece, width), f32),
            pltpu.VMEM((quarter, width), f32),
            pltpu.VMEM((n_row, quarter, width), bf16),
            dma(()),
            dma(()),
            dma((2 * n_y,)),
            dma((n_row,)),
            dma((2 * n_y,)),
            dma((n_row,)),
            dma((2 + n_fast - 1 + 2 * (SLOW - 1) * n_fast,)),
            dma((n_col,)),
            dma((SLOW * n_fast,)),
            dma((SLOW * n_fast,)),
            dma((n_fast,)),
            dma((n_fast,)),
            dma((SLOW * (n_fast - 1),)),
            dma((SLOW * (n_fast - 1),)),
            dma((SLOW,)),
            dma((SLOW,)),
            dma((n_y,)),
            dma((n_y,)),
            dma((n_y,)),
            dma((n_y,)),
            dma((2 * n_row + 2 * n_col,)),
            dma((n_row,)),
            dma((n_col,)),
            dma((n_col,)),
            dma((n_row,)),
        ],
        compiler_params=pltpu.CompilerParams(
            collective_id=0, has_side_effects=True, vmem_limit_bytes=56 * MB
        ),
        name="layer",
    )(tile_live.reshape(-1), coords, row_degree, col_degree, features, weight, cotangent, tile_edges[0, 0])
    return pl.pallas_call(
        hand_over_kernel,
        out_shape=tuple(shape(r.shape, r.dtype) for r in results),
        in_specs=vmem(3),
        out_specs=tuple(vmem(3)),
        compiler_params=pltpu.CompilerParams(vmem_limit_bytes=60 * MB),
        name="hand_over",
    )(*results)


def solution(mesh):
    in_specs = (
        P(("col", "row"), None),
        P(),
        P("row", "col", None, None),
        P("row", "col"),
        P("row", "col", None, None, None),
        P(("row", "col")),
        P(("col", "row")),
        P(("row", "col"), None),
    )
    out_specs = (P(("row", "col"), None), P(("col", "row"), None), P())
    body = functools.partial(shards, mesh.shape["row"], mesh.shape["col"])
    return jax.shard_map(body, mesh=mesh, in_specs=in_specs, out_specs=out_specs, check_vma=False)
```
